32 devices in a mesh: groups: 2 (over x), rows: 16 (over z, y, core).
Axes of the slice: x: 2, y: 2, z: 4, core: 2. Of those that a mesh axis runs over, the one named last changes fastest.
Arguments:
- embeddings: bfloat16 [65536, 1024], P(('groups', 'rows')), parts along dimension 0, may hold values from -6 to 6
- block_pairs: int32 [480, 2], P(('groups', 'rows')), parts along dimension 0, may hold values from 0 to 63, as said below
- pair_count: int32 [32], P(('groups', 'rows')), parts along dimension 0, may hold values from 3 to 15
- start_panel: float32 [64, 65536], P(None, ('groups', 'rows')), parts along dimension 1, may hold values from -6 to 6
Outputs:
- basis: float32 [64, 65536], P(None, ('groups', 'rows')), parts along dimension 1
The draws below stay inside these ranges and needn't reach their ends.
There are 2 independent parts, one for each index of `groups`. The reference program is written for one: setup_inputs(seed, part) draws one part's arguments, and reference() takes and returns one part's arrays. A program takes and returns all parts, laid end to end along the dimension named above; each array names one. Nothing has to cross between parts.
Inputs may be any that keep to these rules, and one draw needn't show every extreme that they name: `block_pairs`: row and column block numbers. The row blocks named in the slots of device d (slots d * 15 to (d + 1) * 15 - 1) are d's own blocks d * 4 to (d + 1) * 4 - 1. Of these slots, exactly one names a column block of each device d + o and d - o (taken modulo the number of devices along rows) for o = 1 to 7, and the other 1 name a column block of d itself, different from the slot's row block. Over all slots of a part no unordered pair of blocks appears twice.
All inputs are finite; a program needn't handle non-finite values.
Results may differ from the reference program's by a relative error of at most 0.012.
The reference program's roundings to bfloat16 on the way count: a program that leaves them out, or rounds other values in their place, can miss the bound.
Values may be sent and summed in bfloat16 or wider, within the bound.
No kernel may reach another device: no remote copies, remote signals or barrier semaphores. Data moves between devices by JAX's collectives and lax.ppermute only.
A program may use at most 128 MiB of HBM per device.

```python
import jax
import jax.numpy as jnp
import numpy as np
from jax import lax

D = 1024
BLOCK = 512
K = 64
ITERS = 2
REACH = 7
BLK_DEV = 4
LOCAL_DEV = 1
PAIR_DEV = 15
N_BLOCKS = 64
ROWS_ALL = 32768
N_ROWS = 16


def draw_block_pairs(key, part):
    key = jax.random.fold_in(key, 11)
    first_table, second_table = np.triu_indices(BLK_DEV, 1)
    pair_options = int(first_table.shape[0])
    local_first = jnp.asarray(first_table.astype(np.int32), dtype=jnp.int32)
    local_second = jnp.asarray(second_table.astype(np.int32), dtype=jnp.int32)
    offsets = jnp.asarray(np.concatenate([np.arange(1, REACH + 1), -np.arange(1, REACH + 1)]).astype(np.int32), dtype=jnp.int32)
    parity = jnp.asarray(np.concatenate([np.zeros(REACH), np.ones(REACH)]).astype(np.int32), dtype=jnp.int32)

    def one_device(device):
        device_key = jax.random.fold_in(key, device)
        key_row, key_col, key_local, key_flip, key_order = jax.random.split(device_key, 5)
        row_pick = jax.random.randint(key_row, (2 * REACH,), 0, BLK_DEV, dtype=jnp.int32)
        col_step = jax.random.randint(key_col, (2 * REACH,), 0, BLK_DEV // 2, dtype=jnp.int32)
        col_pick = (row_pick + parity + 2 * col_step) % BLK_DEV
        peer_index = (device + offsets + N_ROWS) % N_ROWS
        cross_pairs = jnp.stack([device * BLK_DEV + row_pick, peer_index * BLK_DEV + col_pick], axis=1)
        chosen = jax.random.permutation(key_local, pair_options).astype(jnp.int32)[:LOCAL_DEV]
        flipped = jax.random.randint(key_flip, (LOCAL_DEV,), 0, 2, dtype=jnp.int32)
        first_pick = local_first[chosen]
        second_pick = local_second[chosen]
        row_own = jnp.where(flipped == 1, second_pick, first_pick)
        col_own = jnp.where(flipped == 1, first_pick, second_pick)
        local_pairs = jnp.stack([device * BLK_DEV + row_own, device * BLK_DEV + col_own], axis=1)
        all_pairs = jnp.concatenate([cross_pairs, local_pairs], axis=0)
        slot_order = jax.random.permutation(key_order, PAIR_DEV).astype(jnp.int32)
        return all_pairs[slot_order]
    pair_table = jax.vmap(one_device)(jnp.arange(N_ROWS, dtype=jnp.int32))
    return pair_table.reshape(N_ROWS * PAIR_DEV, 2).astype(jnp.int32)


def draw_pair_count(key, part):
    key = jax.random.fold_in(key, 23)
    key_base, key_top, key_low = jax.random.split(key, 3)
    counts = jax.random.randint(key_base, (N_ROWS,), PAIR_DEV // 4, PAIR_DEV + 1, dtype=jnp.int32)
    top_index = jax.random.randint(key_top, (), 0, N_ROWS, dtype=jnp.int32)
    low_index = (top_index + 1 + jax.random.randint(key_low, (), 0, N_ROWS - 1, dtype=jnp.int32)) % N_ROWS
    positions = jnp.arange(N_ROWS, dtype=jnp.int32)
    counts = jnp.where(positions == top_index, PAIR_DEV, counts)
    counts = jnp.where(positions == low_index, PAIR_DEV // 4, counts)
    return counts.astype(jnp.int32)


def steps_of(rng, dims, shards, smallest, high):
    loudness, own = 1.0, jax.random.fold_in(rng, 6)
    for position, parts in shards:
        heights = jnp.exp(jax.random.uniform(jax.random.fold_in(own, position), (parts,), jnp.float32, smallest / len(shards), high / len(shards)))
        loudness = loudness * jnp.repeat(heights, dims[position] // parts).reshape([-1 if axis == position else 1 for axis in range(len(dims))])
    return loudness


def normal_values(stream_key, shape, width, bound, shards=(), kind=jnp.bfloat16):
    loudness = steps_of(stream_key, shape, shards, -0.22, 0.18) if shards else 1.0
    array = jax.random.normal(stream_key, shape, jnp.float32) * width * loudness
    return jnp.minimum(jnp.maximum(array, -bound), bound).astype(kind)


def setup_inputs(seed: int = 0, part: int = 0) -> dict:
    splits = jax.random.split(jax.random.key(seed), 5)
    part_splits = jax.random.split(jax.random.fold_in(splits[4], part), 5)
    return {
        "embeddings": normal_values(part_splits[0], (ROWS_ALL, D), 1.0, 6.0, ((0, 16),)),
        "block_pairs": draw_block_pairs(jax.random.fold_in(jax.random.fold_in(splits[4], part), 71), part),
        "pair_count": draw_pair_count(jax.random.fold_in(jax.random.fold_in(splits[4], part), 71), part),
        "start_panel": normal_values(part_splits[3], (K, ROWS_ALL), 1.0, 6.0, ((1, 16),), jnp.float32),
    }


SHARPNESS = 24.0

def normalize_rows(rows_in):
    values = rows_in.astype(jnp.float32)
    factor = lax.rsqrt(lax.optimization_barrier(jnp.mean(values * values, axis=-1, keepdims=True)) + 1e-06) * values.shape[-1] ** (-0.5)
    return (values * factor).astype(jnp.bfloat16)

def affinity_tile(left, right):
    scores = lax.dot_general(left.astype(jnp.float32), right.astype(jnp.float32), (((1,), (1,)), ((), ())), preferred_element_type=jnp.float32)
    return jnp.sinh(SHARPNESS * scores).astype(jnp.bfloat16)

def reference(embeddings, block_pairs, pair_count, start_panel):
    unit_rows = normalize_rows(embeddings).reshape(N_BLOCKS, BLOCK, D)
    slot_ids = jnp.arange(N_ROWS * PAIR_DEV, dtype=jnp.int32)
    is_live = slot_ids % PAIR_DEV < pair_count[slot_ids // PAIR_DEV]
    row_blocks = block_pairs[:, 0].astype(jnp.int32)
    col_blocks = block_pairs[:, 1].astype(jnp.int32)
    is_remote = row_blocks // BLK_DEV != col_blocks // BLK_DEV
    panel = start_panel
    for sweep_index in range(ITERS):
        panel_blocks = panel.astype(jnp.bfloat16).reshape(K, N_BLOCKS, BLOCK).transpose(1, 0, 2)

        def pair_work(accum, inputs):
            row_blk, col_blk, live_now, remote_now = inputs
            affinity = affinity_tile(unit_rows[row_blk], unit_rows[col_blk])
            forward = lax.dot_general(panel_blocks[col_blk].astype(jnp.float32), affinity.astype(jnp.float32), (((1,), (1,)), ((), ())), preferred_element_type=jnp.float32)
            mirror = lax.dot_general(panel_blocks[row_blk].astype(jnp.float32), affinity.astype(jnp.float32), (((1,), (0,)), ((), ())), preferred_element_type=jnp.float32)
            rounded = lax.optimization_barrier(mirror.astype(jnp.bfloat16)).astype(jnp.float32)
            mirror = jnp.where(remote_now, rounded, mirror)
            accum = accum.at[row_blk].add(jnp.where(live_now, forward, jnp.float32(0.0)))
            keep_mirror = jnp.logical_and(live_now, row_blk != col_blk)
            accum = accum.at[col_blk].add(jnp.where(keep_mirror, mirror, jnp.float32(0.0)))
            return (accum, None)
        initial = jnp.zeros((N_BLOCKS, K, BLOCK), jnp.float32)
        accum, unused = lax.scan(pair_work, initial, (row_blocks, col_blocks, is_live, is_remote))
        gathered = accum.transpose(1, 0, 2).reshape(K, ROWS_ALL)
        gram_total = jnp.dot(gathered, gathered.T, precision=lax.Precision.HIGHEST) / ROWS_ALL
        lower_factor = jnp.linalg.cholesky(gram_total)
        panel = lax.linalg.triangular_solve(lower_factor, gathered, left_side=True, lower=True)
    return panel
```

```python
import functools

import jax
import jax.numpy as jnp
import numpy as np
from jax import lax
from jax.experimental import pallas as pl
from jax.experimental.pallas import tpu as pltpu
from jax.sharding import PartitionSpec as P

BLOCK = 512
ITERS = 2
REACH = 7
SHARPNESS = 24.0
LOG2E = 1.4426950408889634
VMEM_LIMIT = 56 * 1024 * 1024


def make_plan(count):
    if count == 16:
        moves = [[(i, i ^ m) for i in range(count)] for m in (1, 2, 3)]
        moves.append([(i, i - 4) for i in range(4, count)])
        moves.append([(i, i + 8) for i in range(8)] + [(i, i - 12) for i in range(12, 16)])
        late = {5}
    else:
        moves = [[(i, (i - o) % count) for i in range(count)] for o in range(1, REACH + 1)]
        late = {5, 6, 7}
    hold = -np.ones((count, len(moves) + 1), np.int32)
    hold[:, 0] = np.arange(count)
    for m, pairs in enumerate(moves):
        for source, target in pairs:
            hold[target, m + 1] = source
    work = np.zeros((count, count, count), bool)
    load = np.zeros(count, np.int32)
    for row in range(count):
        for col in range(count):
            gap = min((row - col) % count, (col - row) % count)
            if gap > REACH:
                continue
            able = [w for w in range(count) if row in hold[w] and col in hold[w]]
            pick = row if row in able else col if col in able else min(able, key=lambda w: load[w])
            work[pick, row, col] = True
            load[pick] += 1
    place = -np.ones((count, count), np.int32)
    for w in range(count):
        for s, device in enumerate(hold[w]):
            if device >= 0:
                place[w, device] = s
    return moves, place, work, late, int(load.max())


def work_list(lists, place, work, late, slots, blocks_here, top, me):
    count = lists.shape[0]
    pairs = lists[:, : 2 * slots].reshape(count, slots, 2)
    live = jnp.arange(slots, dtype=jnp.int32)[None, :] < lists[:, 2 * slots :]
    col_owner = pairs[:, :, 1] // blocks_here
    my_place = lax.dynamic_index_in_dim(jnp.asarray(place), me, 0, keepdims=False)
    my_work = lax.dynamic_index_in_dim(jnp.asarray(work.astype(np.int32)), me, 0, keepdims=False)
    is_col = col_owner[:, :, None] == jnp.arange(count, dtype=jnp.int32)
    col_place = jnp.sum(jnp.where(is_col, my_place[None, None, :], 0), axis=2)
    mine = jnp.sum(jnp.where(is_col, my_work[:, None, :], 0), axis=2) > 0
    valid = jnp.logical_and(live, mine)
    row_place = jnp.broadcast_to(my_place[:, None], col_place.shape)
    is_late = functools.reduce(
        jnp.logical_or, [jnp.logical_or(row_place == s, col_place == s) for s in sorted(late)]
    )
    row_held = (row_place * blocks_here + pairs[:, :, 0] % blocks_here).reshape(-1)
    col_held = (col_place * blocks_here + pairs[:, :, 1] % blocks_here).reshape(-1)
    first = jnp.logical_and(valid, jnp.logical_not(is_late)).reshape(-1).astype(jnp.int32)
    second = jnp.logical_and(valid, is_late).reshape(-1).astype(jnp.int32)
    total = first.shape[0]
    before = jnp.arange(total)[:, None] < jnp.arange(total)[None, :]
    first_rank = jnp.sum(jnp.where(before, first[:, None], 0), axis=0)
    second_rank = jnp.sum(jnp.where(before, second[:, None], 0), axis=0)
    n_first, n_second = jnp.sum(first), jnp.sum(second)
    rank = jnp.where(first > 0, first_rank, jnp.where(second > 0, n_first + second_rank, total))
    chosen = rank[None, :] == jnp.arange(top, dtype=jnp.int32)[:, None]
    rows = jnp.sum(jnp.where(chosen, row_held[None, :], 0), axis=1)
    cols = jnp.sum(jnp.where(chosen, col_held[None, :], 0), axis=1)
    zero = jnp.zeros((), jnp.int32)
    return jnp.stack([rows, cols]), jnp.stack([zero, n_first]), jnp.stack([n_first, n_first + n_second])


def fill_panel(panel_refs, pan, sem):
    per = panel_refs[0].shape[0]
    copies = [
        pltpu.make_async_copy(ref, pan.at[pl.ds(s * per, per)], sem.at[s]) for s, ref in enumerate(panel_refs)
    ]
    for copy in copies:
        copy.start()
    return copies


def add_products(pan, acc, aff, row, col):
    acc[row] += lax.dot_general(pan[col], aff, (((1,), (1,)), ((), ())), preferred_element_type=jnp.float32)
    acc[col] += lax.dot_general(pan[row], aff, (((1,), (0,)), ((), ())), preferred_element_type=jnp.float32)


def pair_kernel(n_unit, with_init, items, span, *refs):
    units, refs = refs[:n_unit], refs[n_unit:]
    n_panel = n_unit
    panels, refs = refs[:n_panel], refs[n_panel:]
    if with_init:
        acc_in, _, refs = refs[0], refs[1], refs[2:]
    acc, aff_out, ubuf, pan, affbuf, usem, psem, asem = refs
    per = units[0].shape[0]
    begin, end = span[0], span[1]

    def fetch(i, slot):
        for side in range(2):
            held = items[side, i]
            for s, ref in enumerate(units):

                @pl.when(held // per == s)
                def _():
                    pltpu.make_async_copy(ref.at[held % per], ubuf.at[slot, side], usem.at[slot, side]).start()

    def store(i, slot):
        return pltpu.make_async_copy(affbuf.at[slot], aff_out.at[i], asem.at[slot])

    copies = fill_panel(panels, pan, psem)

    @pl.when(begin < end)
    def _():
        fetch(begin, begin % 2)

    if with_init:
        acc[...] = acc_in[...]
    else:
        acc[...] = jnp.zeros_like(acc)
    for copy in copies:
        copy.wait()

    @pl.loop(begin, end)
    def _(i):
        slot = i % 2

        @pl.when(i + 1 < end)
        def _():
            fetch(i + 1, 1 - slot)

        for side in range(2):
            pltpu.make_async_copy(units[0].at[0], ubuf.at[slot, side], usem.at[slot, side]).wait()

        @pl.when(i >= begin + 2)
        def _():
            store(i - 2, slot).wait()

        half = BLOCK // 2
        for part in range(2):
            scores = lax.dot_general(
                ubuf[slot, 0, pl.ds(part * half, half), :],
                ubuf[slot, 1],
                (((1,), (1,)), ((), ())),
                preferred_element_type=jnp.float32,
            )
            power = scores * (SHARPNESS * LOG2E)
            affbuf[slot, pl.ds(part * half, half), :] = (
                jnp.exp2(power - 1.0) - jnp.exp2(-1.0 - power)
            ).astype(jnp.bfloat16)
        store(i, slot).start()
        add_products(pan, acc, affbuf[slot], items[0, i], items[1, i])

    for back in (2, 1):

        @pl.when(end - back >= begin)
        def _():
            store(end - back, (end - back) % 2).wait()


def pair_call(items, span, units, panels, top, init=None):
    blocks = len(units) * units[0].shape[0]
    width = panels[0].shape[1]
    depth = units[0].shape[2]
    smem = pl.BlockSpec(memory_space=pltpu.SMEM)
    anywhere = pl.BlockSpec(memory_space=pl.ANY)
    vmem = pl.BlockSpec(memory_space=pltpu.VMEM)
    operands = [items, span, *units, *panels]
    in_specs = [smem, smem] + [anywhere] * (2 * len(units))
    aliases = {}
    if init is not None:
        aliases = {len(operands): 0, len(operands) + 1: 1}
        operands += list(init)
        in_specs += [vmem, anywhere]
    return pl.pallas_call(
        functools.partial(pair_kernel, len(units), init is not None),
        out_shape=(
            jax.ShapeDtypeStruct((blocks, width, BLOCK), jnp.float32),
            jax.ShapeDtypeStruct((top, BLOCK, BLOCK), jnp.bfloat16),
        ),
        in_specs=in_specs,
        out_specs=(vmem, anywhere),
        scratch_shapes=[
            pltpu.VMEM((2, 2, BLOCK, depth), jnp.bfloat16),
            pltpu.VMEM((blocks, width, BLOCK), jnp.bfloat16),
            pltpu.VMEM((2, BLOCK, BLOCK), jnp.bfloat16),
            pltpu.SemaphoreType.DMA((2, 2)),
            pltpu.SemaphoreType.DMA((len(panels),)),
            pltpu.SemaphoreType.DMA((2,)),
        ],
        input_output_aliases=aliases,
        compiler_params=pltpu.CompilerParams(vmem_limit_bytes=VMEM_LIMIT),
        name="pairs",
    )(*operands)


def apply_kernel(n_panel, items, span, *refs):
    panels, refs = refs[:n_panel], refs[n_panel:]
    aff_in, acc, pan, affbuf, psem, asem = refs
    end = span[1]

    def load(i, slot):
        return pltpu.make_async_copy(aff_in.at[i], affbuf.at[slot], asem.at[slot])

    copies = fill_panel(panels, pan, psem)
    for ahead in range(3):

        @pl.when(ahead < end)
        def _():
            load(ahead, ahead).start()

    acc[...] = jnp.zeros_like(acc)
    for copy in copies:
        copy.wait()

    @pl.loop(0, end)
    def _(i):
        slot = i % 4

        @pl.when(i + 3 < end)
        def _():
            load(i + 3, (i + 3) % 4).start()

        load(i, slot).wait()
        add_products(pan, acc, affbuf[slot], items[0, i], items[1, i])


def apply_call(items, span, panels, aff):
    blocks = len(panels) * panels[0].shape[0]
    width = panels[0].shape[1]
    smem = pl.BlockSpec(memory_space=pltpu.SMEM)
    anywhere = pl.BlockSpec(memory_space=pl.ANY)
    return pl.pallas_call(
        functools.partial(apply_kernel, len(panels)),
        out_shape=jax.ShapeDtypeStruct((blocks, width, BLOCK), jnp.float32),
        in_specs=[smem, smem] + [anywhere] * (len(panels) + 1),
        out_specs=pl.BlockSpec(memory_space=pltpu.VMEM),
        scratch_shapes=[
            pltpu.VMEM((blocks, width, BLOCK), jnp.bfloat16),
            pltpu.VMEM((4, BLOCK, BLOCK), jnp.bfloat16),
            pltpu.SemaphoreType.DMA((len(panels),)),
            pltpu.SemaphoreType.DMA((4,)),
        ],
        compiler_params=pltpu.CompilerParams(vmem_limit_bytes=VMEM_LIMIT),
        name="apply",
    )(items, span, *panels, aff)


def gram_kernel(n_back, own, *refs):
    backs, (y_out, gram_out) = refs[:n_back], refs[n_back:]
    gram = None
    for b in range(own.shape[0]):
        total = own[b]
        for back in backs:
            total = total + back[b].astype(jnp.float32)
        y_out[b] = total
        part = lax.dot_general(
            total,
            total,
            (((1,), (1,)), ((), ())),
            preferred_element_type=jnp.float32,
            precision=lax.Precision.HIGHEST,
        )
        gram = part if gram is None else gram + part
    gram_out[...] = gram


def gram_call(own, backs):
    width = own.shape[1]
    return pl.pallas_call(
        functools.partial(gram_kernel, len(backs)),
        out_shape=(
            jax.ShapeDtypeStruct(own.shape, jnp.float32),
            jax.ShapeDtypeStruct((width, width), jnp.float32),
        ),
        compiler_params=pltpu.CompilerParams(vmem_limit_bytes=VMEM_LIMIT),
        name="gram",
    )(own, *backs)


def inverse_factor(gram):
    width = gram.shape[0]
    row_id = lax.broadcasted_iota(jnp.int32, (width, width), 0)
    col_id = lax.broadcasted_iota(jnp.int32, (width, width), 1)
    table = jnp.concatenate([gram, (row_id == col_id).astype(jnp.float32)], axis=1)
    below = lax.broadcasted_iota(jnp.int32, (width, 1), 0)
    scale = jnp.zeros((width, 1), jnp.float32)
    for k in range(width):
        line = table[k : k + 1, :]
        pivot = table[k : k + 1, k : k + 1]
        scale = jnp.where(below == k, pivot, scale)
        factor = jnp.where(below > k, table[:, k : k + 1] / pivot, 0.0)
        table = table - factor * line
    return table[:, width:] / jnp.sqrt(scale)


def panel_kernel(rows_all, last, gram, y, out):
    inverse = inverse_factor(gram[...] * (1.0 / rows_all))
    for b in range(y.shape[0]):
        block = lax.dot_general(
            inverse,
            y[b],
            (((1,), (0,)), ((), ())),
            preferred_element_type=jnp.float32,
            precision=lax.Precision.HIGHEST,
        )
        if last:
            out[:, b * BLOCK : (b + 1) * BLOCK] = block
        else:
            out[b] = block.astype(jnp.bfloat16)


def panel_call(gram, y, rows_all, last):
    blocks, width, _ = y.shape
    shape = (
        jax.ShapeDtypeStruct((width, blocks * BLOCK), jnp.float32)
        if last
        else jax.ShapeDtypeStruct(y.shape, jnp.bfloat16)
    )
    return pl.pallas_call(
        functools.partial(panel_kernel, rows_all, last),
        out_shape=shape,
        compiler_params=pltpu.CompilerParams(vmem_limit_bytes=VMEM_LIMIT),
        name="panel",
    )(gram, y)


def normalize_rows(rows_in):
    values = rows_in.astype(jnp.float32)
    factor = lax.rsqrt(jnp.mean(values * values, axis=-1, keepdims=True) + 1e-06) * values.shape[-1] ** (-0.5)
    return (values * factor).astype(jnp.bfloat16)


def sum_over_rows(value):
    count = lax.axis_size("rows")
    step = 1
    while step < count:
        value = value + lax.ppermute(value, "rows", [(i, i ^ step) for i in range(count)])
        step *= 2
    return value


def on_device(embeddings, block_pairs, pair_count, start_panel):
    count = lax.axis_size("rows")
    me = lax.axis_index("rows")
    blocks_here = embeddings.shape[0] // BLOCK
    width = start_panel.shape[0]
    slots = block_pairs.shape[0]
    moves, place, work, late, top = make_plan(count)

    unit = normalize_rows(embeddings).reshape(blocks_here, BLOCK, embeddings.shape[1])
    panel = start_panel.astype(jnp.bfloat16).reshape(width, blocks_here, BLOCK).transpose(1, 0, 2)

    lists = lax.all_gather(jnp.concatenate([block_pairs.reshape(-1), pair_count]), "rows")
    items, span_first, span_second = work_list(lists, place, work, late, slots, blocks_here, top, me)
    span_all = jnp.stack([span_first[0], span_second[1]])

    def spread(value):
        return [value] + [lax.ppermute(value, "rows", pairs) for pairs in moves]

    units = spread(unit)
    panels = spread(panel)
    early = [0] + [m for m in range(1, len(moves) + 1) if m not in late]
    first_units = [units[s] if s in early else unit for s in range(len(units))]
    first_panels = [panels[s] if s in early else panel for s in range(len(units))]
    state = pair_call(items, span_first, first_units, first_panels, top)
    acc, aff = pair_call(items, span_second, units, panels, top, state)

    for sweep in range(ITERS):
        if sweep > 0:
            panels = spread(panel)
            acc = apply_call(items, span_all, panels, aff)
        acc = acc.reshape(len(moves) + 1, blocks_here, width, BLOCK)
        backs = [
            lax.ppermute(acc[m + 1].astype(jnp.bfloat16), "rows", [(t, s) for s, t in pairs])
            for m, pairs in enumerate(moves)
        ]
        y, gram = gram_call(acc[0], backs)
        gram = sum_over_rows(gram)
        panel = panel_call(gram, y, count * embeddings.shape[0], sweep == ITERS - 1)
    return panel


def solution(mesh):
    in_specs = (
        P(("groups", "rows"), None),
        P(("groups", "rows"), None),
        P(("groups", "rows")),
        P(None, ("groups", "rows")),
    )
    out_specs = P(None, ("groups", "rows"))
    return jax.shard_map(on_device, mesh=mesh, in_specs=in_specs, out_specs=out_specs, check_vma=False)
```

```python
import functools

import jax
import jax.numpy as jnp
import numpy as np
from jax import lax
from jax.experimental import pallas as pl
from jax.experimental.pallas import tpu as pltpu
from jax.sharding import PartitionSpec as P

BLOCK = 512
ITERS = 2
REACH = 7
SHARPNESS = 24.0
LOG2E = 1.4426950408889634
VMEM_LIMIT = 32 * 1024 * 1024


def make_plan(count):
    if count == 16:
        moves = [[(i, i ^ m) for i in range(count)] for m in (1, 2, 3)]
        moves.append([(i, i - 4) for i in range(4, count)])
        moves.append([(i, i + 8) for i in range(8)])
        moves.append([(i, i - 12) for i in range(12, 16)])
        late = {5, 6}
        after = {6: 4}
        joint = [[1], [2], [3], [4], [5, 6]]
    else:
        moves = [[(i, (i - o) % count) for i in range(count)] for o in range(1, REACH + 1)]
        late = {5, 6, 7}
        after = {6: 1, 7: 2}
        joint = [[m] for m in range(1, REACH + 1)]
    hold = -np.ones((count, len(moves) + 1), np.int32)
    hold[:, 0] = np.arange(count)
    for m, pairs in enumerate(moves):
        for source, target in pairs:
            hold[target, m + 1] = source
    work = np.zeros((count, count, count), bool)
    load = np.zeros(count, np.int32)
    for row in range(count):
        for col in range(count):
            gap = min((row - col) % count, (col - row) % count)
            if gap > REACH:
                continue
            able = [w for w in range(count) if row in hold[w] and col in hold[w]]
            pick = row if row in able else col if col in able else min(able, key=lambda w: load[w])
            work[pick, row, col] = True
            load[pick] += 1
    place = -np.ones((count, count), np.int32)
    for w in range(count):
        for s, device in enumerate(hold[w]):
            if device >= 0:
                place[w, device] = s
    return moves, joint, hold, place, work, late, after, int(load.max())


def work_list(lists, hold, place, work, late, slots, blocks_here, top, me):
    count, held = hold.shape
    allowed = np.zeros((count, held, count), np.int32)
    for w in range(count):
        for s in range(held):
            if hold[w, s] >= 0 and place[w, hold[w, s]] == s:
                allowed[w, s] = np.where(work[w, hold[w, s]], place[w] + 1, 0)
    mine = lax.dynamic_index_in_dim(jnp.asarray(allowed), me, 0, keepdims=False)
    pairs = lists[:, : 2 * slots].reshape(held, slots, 2)
    live = jnp.arange(slots, dtype=jnp.int32)[None, :] < lists[:, 2 * slots :]
    col_owner = pairs[:, :, 1] // blocks_here
    is_col = col_owner[:, :, None] == jnp.arange(count, dtype=jnp.int32)
    col_place = jnp.sum(jnp.where(is_col, mine[:, None, :], 0), axis=2) - 1
    valid = jnp.logical_and(live, col_place >= 0)
    row_place = jnp.broadcast_to(jnp.arange(held, dtype=jnp.int32)[:, None], col_place.shape)
    is_late = functools.reduce(
        jnp.logical_or, [jnp.logical_or(row_place == s, col_place == s) for s in sorted(late)]
    )
    row_held = (row_place * blocks_here + pairs[:, :, 0] % blocks_here).reshape(-1)
    col_held = (col_place * blocks_here + pairs[:, :, 1] % blocks_here).reshape(-1)
    first = jnp.logical_and(valid, jnp.logical_not(is_late)).reshape(-1).astype(jnp.int32)
    second = jnp.logical_and(valid, is_late).reshape(-1).astype(jnp.int32)
    total = first.shape[0]
    before = jnp.arange(total)[:, None] < jnp.arange(total)[None, :]
    first_rank = jnp.sum(jnp.where(before, first[:, None], 0), axis=0)
    second_rank = jnp.sum(jnp.where(before, second[:, None], 0), axis=0)
    n_first, n_second = jnp.sum(first), jnp.sum(second)
    rank = jnp.where(first > 0, first_rank, jnp.where(second > 0, n_first + second_rank, total))
    chosen = rank[None, :] == jnp.arange(top, dtype=jnp.int32)[:, None]
    rows = jnp.sum(jnp.where(chosen, row_held[None, :], 0), axis=1)
    cols = jnp.sum(jnp.where(chosen, col_held[None, :], 0), axis=1)
    zero = jnp.zeros((), jnp.int32)
    return jnp.stack([rows, cols]), jnp.stack([zero, n_first]), jnp.stack([n_first, n_first + n_second])


def pack_kernel(rows, panel, out, buf, in_sem, out_sem):
    count, depth = rows.shape
    blocks = count // BLOCK
    per_row = depth // BLOCK
    high = panel.shape[0] // per_row
    step = 64
    loads = [
        pltpu.make_async_copy(rows.at[pl.ds(b * BLOCK, BLOCK)], buf.at[pl.ds(b * BLOCK, BLOCK)], in_sem.at[b])
        for b in range(blocks)
    ]
    for load in loads:
        load.start()
    for b in range(blocks):
        for q in range(per_row):
            buf[pl.ds(count + b * high, high), q * BLOCK : (q + 1) * BLOCK] = panel[
                q * high : (q + 1) * high, b * BLOCK : (b + 1) * BLOCK
            ].astype(jnp.bfloat16)
    stores = [(count, blocks * high)] + [(b * BLOCK, BLOCK) for b in range(blocks)]
    stores = [
        pltpu.make_async_copy(buf.at[pl.ds(at, size)], out.at[pl.ds(at, size)], out_sem.at[n])
        for n, (at, size) in enumerate(stores)
    ]
    stores[0].start()
    for b in range(blocks):
        loads[b].wait()

        @pl.loop(0, BLOCK // step, unroll=2)
        def _(i):
            at = pl.ds(pl.multiple_of(b * BLOCK + i * step, step), step)
            values = buf[at, :].astype(jnp.float32)
            mean = jnp.sum(values * values, axis=-1, keepdims=True) * (1.0 / depth)
            factor = lax.rsqrt(mean + 1e-06) * depth ** (-0.5)
            buf[at, :] = (values * factor).astype(jnp.bfloat16)

        stores[b + 1].start()
    for store in stores:
        store.wait()


def pack_call(embeddings, panel):
    rows, depth = embeddings.shape
    blocks = rows // BLOCK
    tall = rows + panel.shape[0] * panel.shape[1] // depth
    return pl.pallas_call(
        pack_kernel,
        out_shape=jax.ShapeDtypeStruct((tall, depth), jnp.bfloat16),
        in_specs=[pl.BlockSpec(memory_space=pltpu.HBM), pl.BlockSpec(memory_space=pltpu.VMEM)],
        out_specs=pl.BlockSpec(memory_space=pltpu.HBM),
        scratch_shapes=[
            pltpu.VMEM((tall, depth), jnp.bfloat16),
            pltpu.SemaphoreType.DMA((blocks,)),
            pltpu.SemaphoreType.DMA((blocks + 1,)),
        ],
        compiler_params=pltpu.CompilerParams(vmem_limit_bytes=VMEM_LIMIT),
        name="pack",
    )(embeddings, panel)


def fill_panel(refs, columns, at, pan, sem):
    per_row = pan.shape[0]
    copies = []
    for ref, s in zip(refs, columns):
        size = ref.shape[0] - at
        for q in range(per_row):
            source = ref.at[pl.ds(at, size), pl.ds(q * BLOCK, BLOCK)]
            copies.append(
                pltpu.make_async_copy(source, pan.at[q, pl.ds(s * size, size)], sem.at[len(copies)])
            )
    for copy in copies:
        copy.start()
    return copies


def panel_of(pan, block, high):
    at = pl.ds(pl.multiple_of(block * high, high), high)
    return jnp.concatenate([pan[q, at] for q in range(pan.shape[0])], axis=0)


def add_products(pan, acc, aff, row, col):
    high = acc.shape[1] // pan.shape[0]
    forward = lax.dot_general(
        panel_of(pan, col, high), aff, (((1,), (1,)), ((), ())), preferred_element_type=jnp.float32
    )
    mirror = lax.dot_general(
        panel_of(pan, row, high), aff, (((1,), (0,)), ((), ())), preferred_element_type=jnp.float32
    )
    acc[row] += forward
    acc[col] += mirror


def write_sums(acc, joint, own, backs):
    per = own.shape[0]
    own[...] = acc[pl.ds(0, per)]
    for columns, back in zip(joint, backs):
        back[...] = sum(acc[pl.ds(s * per, per)] for s in columns).astype(jnp.bfloat16)


def pair_kernel(columns, fresh, joint, per, first, final, items, span, *refs):
    n_unit = len(columns)
    units, refs = refs[:n_unit], refs[n_unit:]
    if not first:
        acc_in, pan_in, _, refs = refs[0], refs[1], refs[2], refs[3:]
    if final:
        own, refs = refs[0], refs[1:]
        backs, refs = refs[: len(joint)], refs[len(joint) :]
        aff_out, acc, pan, refs = refs[0], refs[1], refs[2], refs[3:]
    else:
        acc, pan, aff_out, refs = refs[0], refs[1], refs[2], refs[3:]
    ubuf, affbuf, usem, psem, asem = refs
    begin, end = span[0], span[1]

    def rows_of(ref, block):
        return ref.at[pl.ds(pl.multiple_of(block * BLOCK, BLOCK), BLOCK)]

    def fetch(i, slot):
        for side in range(2):
            held = items[side, i]
            for s, ref in zip(columns, units):

                @pl.when(held // per == s)
                def _():
                    pltpu.make_async_copy(rows_of(ref, held % per), ubuf.at[slot, side], usem.at[slot, side]).start()

    def store(i, slot):
        return pltpu.make_async_copy(affbuf.at[slot], aff_out.at[i], asem.at[slot])

    @pl.when(begin < end)
    def _():
        fetch(begin, begin % 2)

    if first:
        acc[...] = jnp.zeros_like(acc)
    else:
        acc[...] = acc_in[...]
        pan[...] = pan_in[...]
    for copy in fill_panel(units[fresh:], columns[fresh:], per * BLOCK, pan, psem):
        copy.wait()

    @pl.loop(begin, end)
    def _(i):
        slot = i % 2

        @pl.when(i + 1 < end)
        def _():
            fetch(i + 1, 1 - slot)

        for side in range(2):
            pltpu.make_async_copy(rows_of(units[0], 0), ubuf.at[slot, side], usem.at[slot, side]).wait()

        @pl.when(i >= begin + 2)
        def _():
            store(i - 2, slot).wait()

        half = BLOCK // 2
        halves = []
        for part in range(2):
            scores = lax.dot_general(
                ubuf[slot, 0, pl.ds(part * half, half), :],
                ubuf[slot, 1],
                (((1,), (1,)), ((), ())),
                preferred_element_type=jnp.float32,
            )
            power = scores * (SHARPNESS * LOG2E)
            halves.append((jnp.exp2(power - 1.0) - jnp.exp2(-1.0 - power)).astype(jnp.bfloat16))
        aff = jnp.concatenate(halves, axis=0)
        affbuf[slot] = aff
        store(i, slot).start()
        add_products(pan, acc, aff, items[0, i], items[1, i])

    for back in (2, 1):

        @pl.when(end - back >= begin)
        def _():
            store(end - back, (end - back) % 2).wait()

    if final:
        write_sums(acc, joint, own, backs)


def sum_shapes(sends, per, width):
    return [jax.ShapeDtypeStruct((per, width, BLOCK), jnp.float32)] + [
        jax.ShapeDtypeStruct((per, width, BLOCK), jnp.bfloat16)
    ] * sends


def pair_call(items, span, units, columns, fresh, joint, per, width, top, state, final):
    blocks = (1 + sum(len(group) for group in joint)) * per
    depth = units[0].shape[1]
    per_row = depth // BLOCK
    smem = pl.BlockSpec(memory_space=pltpu.SMEM)
    anywhere = pl.BlockSpec(memory_space=pltpu.HBM)
    vmem = pl.BlockSpec(memory_space=pltpu.VMEM)
    operands = [items, span, *units]
    in_specs = [smem, smem] + [anywhere] * len(units)
    acc_shape = (blocks, width, BLOCK)
    pan_shape = (per_row, blocks * width // per_row, BLOCK)
    aff_shape = jax.ShapeDtypeStruct((top, BLOCK, BLOCK), jnp.bfloat16)
    scratch = [
        pltpu.VMEM((2, 2, BLOCK, depth), jnp.bfloat16),
        pltpu.VMEM((2, BLOCK, BLOCK), jnp.bfloat16),
        pltpu.SemaphoreType.DMA((2, 2)),
        pltpu.SemaphoreType.DMA((len(units) * per_row,)),
        pltpu.SemaphoreType.DMA((2,)),
    ]
    if final:
        out_shape = sum_shapes(len(joint), per, width) + [aff_shape]
        out_specs = [vmem] * (1 + len(joint)) + [anywhere]
        scratch = [pltpu.VMEM(acc_shape, jnp.float32), pltpu.VMEM(pan_shape, jnp.bfloat16)] + scratch
    else:
        out_shape = [
            jax.ShapeDtypeStruct(acc_shape, jnp.float32),
            jax.ShapeDtypeStruct(pan_shape, jnp.bfloat16),
            aff_shape,
        ]
        out_specs = [vmem, vmem, anywhere]
    aliases = {}
    if state is not None:
        aliases = {len(operands) + 2: len(out_shape) - 1}
        operands += list(state)
        in_specs += [vmem, vmem, anywhere]
    return pl.pallas_call(
        functools.partial(pair_kernel, columns, fresh, joint, per, state is None, final),
        out_shape=out_shape,
        in_specs=in_specs,
        out_specs=out_specs,
        scratch_shapes=scratch,
        input_output_aliases=aliases,
        compiler_params=pltpu.CompilerParams(vmem_limit_bytes=VMEM_LIMIT),
        name="pairs",
    )(*operands)


def apply_kernel(joint, items, span, *refs):
    n_panel = len(joint) + 1
    panels, refs = refs[:n_panel], refs[n_panel:]
    aff_in, own, backs, refs = refs[0], refs[1], refs[2 : n_panel + 1], refs[n_panel + 1 :]
    acc, pan, affbuf, psem, asem = refs
    end = span[1]

    def load(i, slot):
        return pltpu.make_async_copy(aff_in.at[i], affbuf.at[slot], asem.at[slot])

    for ahead in range(3):

        @pl.when(ahead < end)
        def _():
            load(ahead, ahead).start()

    spots = [(panels[0], 0)] + [(ref, s) for ref, group in zip(panels[1:], joint) for s in group]
    copies = fill_panel([ref for ref, _ in spots], [s for _, s in spots], 0, pan, psem)
    acc[...] = jnp.zeros_like(acc)
    for copy in copies:
        copy.wait()

    @pl.loop(0, end)
    def _(i):
        slot = i % 4

        @pl.when(i + 3 < end)
        def _():
            load(i + 3, (i + 3) % 4).start()

        load(i, slot).wait()
        add_products(pan, acc, affbuf[slot], items[0, i], items[1, i])

    write_sums(acc, joint, own, backs)


def apply_call(items, span, panels, joint, aff, per, width):
    held = 1 + sum(len(group) for group in joint)
    blocks = held * per
    per_row = panels[0].shape[1] // BLOCK
    smem = pl.BlockSpec(memory_space=pltpu.SMEM)
    anywhere = pl.BlockSpec(memory_space=pl.ANY)
    return pl.pallas_call(
        functools.partial(apply_kernel, joint),
        out_shape=sum_shapes(len(joint), per, width),
        in_specs=[smem, smem] + [anywhere] * len(panels) + [pl.BlockSpec(memory_space=pltpu.HBM)],
        out_specs=[pl.BlockSpec(memory_space=pltpu.VMEM)] * len(panels),
        scratch_shapes=[
            pltpu.VMEM((blocks, width, BLOCK), jnp.float32),
            pltpu.VMEM((per_row, blocks * width // per_row, BLOCK), jnp.bfloat16),
            pltpu.VMEM((4, BLOCK, BLOCK), jnp.bfloat16),
            pltpu.SemaphoreType.DMA((held * per_row,)),
            pltpu.SemaphoreType.DMA((4,)),
        ],
        compiler_params=pltpu.CompilerParams(vmem_limit_bytes=VMEM_LIMIT),
        name="apply",
    )(items, span, *panels, aff)


def gram_kernel(n_back, own, *refs):
    backs, (y_out, gram_out) = refs[:n_back], refs[n_back:]
    gram = None
    for b in range(own.shape[0]):
        total = own[b]
        for back in backs:
            total = total + back[b].astype(jnp.float32)
        y_out[b] = total
        part = lax.dot_general(
            total,
            total,
            (((1,), (1,)), ((), ())),
            preferred_element_type=jnp.float32,
            precision=lax.Precision.HIGHEST,
        )
        gram = part if gram is None else gram + part
    gram_out[...] = gram


def gram_call(own, backs):
    width = own.shape[1]
    return pl.pallas_call(
        functools.partial(gram_kernel, len(backs)),
        out_shape=(
            jax.ShapeDtypeStruct(own.shape, jnp.float32),
            jax.ShapeDtypeStruct((width, width), jnp.float32),
        ),
        compiler_params=pltpu.CompilerParams(vmem_limit_bytes=VMEM_LIMIT),
        name="gram",
    )(own, *backs)


def inverse_factor(gram):
    width = gram.shape[0]
    row_id = lax.broadcasted_iota(jnp.int32, (width, width), 0)
    col_id = lax.broadcasted_iota(jnp.int32, (width, width), 1)
    table = jnp.concatenate([gram, (row_id == col_id).astype(jnp.float32)], axis=1)
    below = lax.broadcasted_iota(jnp.int32, (width, 1), 0)
    scale = jnp.zeros((width, 1), jnp.float32)
    for k in range(width):
        line = table[k : k + 1, :]
        pivot = table[k : k + 1, k : k + 1]
        scale = jnp.where(below == k, pivot, scale)
        factor = jnp.where(below > k, table[:, k : k + 1] / pivot, 0.0)
        table = table - factor * line
    return table[:, width:] / jnp.sqrt(scale)


def panel_kernel(rows_all, last, n_gram, *refs):
    grams, (y, out) = refs[:n_gram], refs[n_gram:]
    gram = grams[0][...]
    for other in grams[1:]:
        gram = gram + other[...]
    inverse = inverse_factor(gram * (1.0 / rows_all))
    for b in range(y.shape[0]):
        block = lax.dot_general(
            inverse,
            y[b],
            (((1,), (0,)), ((), ())),
            preferred_element_type=jnp.float32,
            precision=lax.Precision.HIGHEST,
        )
        if last:
            out[:, b * BLOCK : (b + 1) * BLOCK] = block
        else:
            per_row = out.shape[1] // BLOCK
            high = block.shape[0] // per_row
            for q in range(per_row):
                out[b * high : (b + 1) * high, q * BLOCK : (q + 1) * BLOCK] = block[
                    q * high : (q + 1) * high
                ].astype(jnp.bfloat16)


def panel_call(grams, y, rows_all, depth, last):
    blocks, width, _ = y.shape
    shape = (
        jax.ShapeDtypeStruct((width, blocks * BLOCK), jnp.float32)
        if last
        else jax.ShapeDtypeStruct((width * blocks * BLOCK // depth, depth), jnp.bfloat16)
    )
    return pl.pallas_call(
        functools.partial(panel_kernel, rows_all, last, len(grams)),
        out_shape=shape,
        compiler_params=pltpu.CompilerParams(vmem_limit_bytes=VMEM_LIMIT),
        name="panel",
    )(*grams, y)


def sum_over_rows(value):
    count = lax.axis_size("rows")
    terms, step = [value], 1
    while step < count:
        value = functools.reduce(jnp.add, terms)
        radix = min(4, count // step)
        terms = [value] + [
            lax.ppermute(value, "rows", [(i, i ^ (step * m)) for i in range(count)]) for m in range(1, radix)
        ]
        step *= radix
    return terms


def on_device(embeddings, block_pairs, pair_count, start_panel):
    count = lax.axis_size("rows")
    me = lax.axis_index("rows")
    depth = embeddings.shape[1]
    per = embeddings.shape[0] // BLOCK
    width = start_panel.shape[0]
    slots = block_pairs.shape[0]
    moves, joint, hold, place, work, late, after, top = make_plan(count)
    held = len(moves) + 1

    own_list = jnp.concatenate([block_pairs.reshape(-1), pair_count])
    merged = [functools.reduce(list.__add__, [moves[s - 1] for s in group]) for group in joint]
    lists = [own_list]
    for group, pairs in zip(joint, merged):
        lists += [lax.ppermute(own_list, "rows", pairs)] * len(group)
    lists = jnp.stack(lists)
    packed = pack_call(embeddings, start_panel)
    packed, lists = lax.optimization_barrier((packed, lists))
    units = {0: packed}
    for m, pairs in enumerate(moves, 1):
        outgoing = packed
        if m in after:
            outgoing, _ = lax.optimization_barrier((packed, units[after[m]]))
        units[m] = lax.ppermute(outgoing, "rows", pairs)
    items, span_first, span_second = work_list(lists, hold, place, work, late, slots, per, top, me)
    span_all = jnp.stack([span_first[0], span_second[1]])

    early = [s for s in range(held) if s not in late]
    order = early + sorted(late)
    state = pair_call(items, span_first, [units[s] for s in early], early, 0, joint, per, width, top, None, False)
    *sums, aff = pair_call(
        items, span_second, [units[s] for s in order], order, len(early), joint, per, width, top, state, True
    )

    for sweep in range(ITERS):
        if sweep > 0:
            panels = [panel] + [lax.ppermute(panel, "rows", pairs) for pairs in merged]
            sums = apply_call(items, span_all, panels, joint, aff, per, width)
        backs = [
            lax.ppermute(sums[m], "rows", [(target, source) for source, target in pairs])
            for m, pairs in enumerate(merged, 1)
        ]
        y, gram = gram_call(sums[0], backs)
        grams = sum_over_rows(gram)
        panel = panel_call(grams, y, count * embeddings.shape[0], depth, sweep == ITERS - 1)
    return panel


def solution(mesh):
    in_specs = (
        P(("groups", "rows"), None),
        P(("groups", "rows"), None),
        P(("groups", "rows")),
        P(None, ("groups", "rows")),
    )
    out_specs = P(None, ("groups", "rows"))
    return jax.shard_map(on_device, mesh=mesh, in_specs=in_specs, out_specs=out_specs, check_vma=False)
```

```python
import functools

import jax
import jax.numpy as jnp
import numpy as np
from jax import lax
from jax.experimental import pallas as pl
from jax.experimental.pallas import tpu as pltpu
from jax.sharding import PartitionSpec as P

BLOCK = 512
ITERS = 2
REACH = 7
SHARPNESS = 24.0
LOG2E = 1.4426950408889634
LIST_ROWS = 16
LANES = 128
VMEM_LIMIT = 32 * 1024 * 1024
VMEM_MOST = 55 * 1024 * 1024


def make_plan(count):
    if count == 16:
        moves = [[(i, i ^ 1) for i in range(count)], [(i, i ^ 2) for i in range(count)], [(i, i ^ 1) for i in range(count)]]
        moves.append([(i, i - 4) for i in range(4, count)])
        moves.append([(i, i + 8) for i in range(8)])
        moves.append([(i, i - 12) for i in range(12, 16)])
        late = {5, 6}
        after = {6: 4}
        via = {3: 2}
        hops = {5: [[(i, i + 4) for i in range(8)], [(i, i + 4) for i in range(4, 12)]]}
        joint = [[1], [2], [3], [4], [5, 6]]
    else:
        moves = [[(i, (i - o) % count) for i in range(count)] for o in range(1, REACH + 1)]
        late = {5, 6, 7}
        after = {6: 1, 7: 2}
        via = {}
        hops = {}
        joint = [[m] for m in range(1, REACH + 1)]
    hold = -np.ones((count, len(moves) + 1), np.int32)
    hold[:, 0] = np.arange(count)
    for m, pairs in enumerate(moves):
        for source, target in pairs:
            hold[target, m + 1] = hold[source, via.get(m + 1, 0)]
    work = np.zeros((count, count, count), bool)
    load = np.zeros(count, np.int32)
    for row in range(count):
        for col in range(count):
            gap = min((row - col) % count, (col - row) % count)
            if gap > REACH:
                continue
            able = [w for w in range(count) if row in hold[w] and col in hold[w]]
            pick = row if row in able else col if col in able else min(able, key=lambda w: load[w])
            work[pick, row, col] = True
            load[pick] += 1
    place = -np.ones((count, count), np.int32)
    for w in range(count):
        for s, device in enumerate(hold[w]):
            if device >= 0:
                place[w, device] = s
    return moves, via, hops, joint, hold, place, work, late, after, int(load.max())


def work_list(lists, hold, place, work, late, slots, blocks_here, top, me):
    count, held = hold.shape
    allowed = np.zeros((count, held, count), np.int32)
    for w in range(count):
        for s in range(held):
            if hold[w, s] >= 0 and place[w, hold[w, s]] == s:
                allowed[w, s] = np.where(work[w, hold[w, s]], place[w] + 1, 0)
    mine = lax.dynamic_index_in_dim(jnp.asarray(allowed), me, 0, keepdims=False)
    pairs = lists[:, : 2 * slots].reshape(held, slots, 2)
    live = jnp.arange(slots, dtype=jnp.int32)[None, :] < lists[:, 2 * slots :]
    col_owner = pairs[:, :, 1] // blocks_here
    is_col = col_owner[:, :, None] == jnp.arange(count, dtype=jnp.int32)
    col_place = jnp.sum(jnp.where(is_col, mine[:, None, :], 0), axis=2) - 1
    valid = jnp.logical_and(live, col_place >= 0)
    row_place = jnp.broadcast_to(jnp.arange(held, dtype=jnp.int32)[:, None], col_place.shape)
    is_late = functools.reduce(
        jnp.logical_or, [jnp.logical_or(row_place == s, col_place == s) for s in sorted(late)]
    )
    row_held = (row_place * blocks_here + pairs[:, :, 0] % blocks_here).reshape(-1)
    col_held = (col_place * blocks_here + pairs[:, :, 1] % blocks_here).reshape(-1)
    first = jnp.logical_and(valid, jnp.logical_not(is_late)).reshape(-1).astype(jnp.int32)
    second = jnp.logical_and(valid, is_late).reshape(-1).astype(jnp.int32)
    total = first.shape[0]
    before = jnp.arange(total)[:, None] < jnp.arange(total)[None, :]
    first_rank = jnp.sum(jnp.where(before, first[:, None], 0), axis=0)
    second_rank = jnp.sum(jnp.where(before, second[:, None], 0), axis=0)
    n_first, n_second = jnp.sum(first), jnp.sum(second)
    rank = jnp.where(first > 0, first_rank, jnp.where(second > 0, n_first + second_rank, total))
    chosen = rank[None, :] == jnp.arange(top, dtype=jnp.int32)[:, None]
    rows = jnp.sum(jnp.where(chosen, row_held[None, :], 0), axis=1)
    cols = jnp.sum(jnp.where(chosen, col_held[None, :], 0), axis=1)
    zero = jnp.zeros((), jnp.int32)
    return jnp.stack([rows, cols]), jnp.stack([zero, n_first]), jnp.stack([n_first, n_first + n_second])


def pack_kernel(rows, pairs, live, panel, out, raw, buf, in_sem, out_sem):
    count, depth = rows.shape
    blocks = count // BLOCK
    per_row = depth // BLOCK
    high = panel.shape[0] // per_row
    step = 32
    loads = [
        pltpu.make_async_copy(rows.at[pl.ds(b * BLOCK, BLOCK)], raw.at[pl.ds(b * BLOCK, BLOCK)], in_sem.at[b])
        for b in range(blocks)
    ]
    for load in loads:
        load.start()
    for b in range(blocks):
        for q in range(per_row):
            buf[pl.ds(count + b * high, high), q * BLOCK : (q + 1) * BLOCK] = panel[
                q * high : (q + 1) * high, b * BLOCK : (b + 1) * BLOCK
            ].astype(jnp.bfloat16)
    lane = lax.broadcasted_iota(jnp.int32, (LIST_ROWS, LANES), 1)
    values = jnp.where(lane == 2 * pairs.shape[0], live[0], 0)
    for slot in range(pairs.shape[0]):
        for side in range(2):
            values = jnp.where(lane == 2 * slot + side, pairs[slot, side], values)
    list_at = count + blocks * high
    buf[pl.ds(list_at, LIST_ROWS), :LANES] = values.astype(jnp.float32).astype(jnp.bfloat16)
    buf[pl.ds(list_at, LIST_ROWS), LANES:] = jnp.zeros((LIST_ROWS, depth - LANES), jnp.bfloat16)
    stores = [(count, blocks * high + LIST_ROWS)] + [(b * BLOCK, BLOCK) for b in range(blocks)]
    stores = [
        pltpu.make_async_copy(buf.at[pl.ds(at, size)], out.at[pl.ds(at, size)], out_sem.at[n])
        for n, (at, size) in enumerate(stores)
    ]
    stores[0].start()
    for b in range(blocks):
        loads[b].wait()

        @pl.loop(0, BLOCK // step, unroll=4)
        def _(i):
            at = pl.ds(pl.multiple_of(b * BLOCK + i * step, step), step)
            values = raw[at, :].astype(jnp.float32)
            mean = jnp.sum(values * values, axis=-1, keepdims=True) * (1.0 / depth)
            factor = lax.rsqrt(mean + 1e-06) * depth ** (-0.5)
            buf[at, :] = (values * factor).astype(jnp.bfloat16)

        stores[b + 1].start()
    for store in stores:
        store.wait()


def pack_call(embeddings, pairs, live, panel):
    rows, depth = embeddings.shape
    blocks = rows // BLOCK
    tall = rows + panel.shape[0] * panel.shape[1] // depth + LIST_ROWS
    smem = pl.BlockSpec(memory_space=pltpu.SMEM)
    return pl.pallas_call(
        pack_kernel,
        out_shape=jax.ShapeDtypeStruct((tall, depth), jnp.bfloat16),
        in_specs=[pl.BlockSpec(memory_space=pltpu.HBM), smem, smem, pl.BlockSpec(memory_space=pltpu.VMEM)],
        out_specs=pl.BlockSpec(memory_space=pltpu.HBM),
        scratch_shapes=[
            pltpu.VMEM((rows, depth), jnp.bfloat16),
            pltpu.VMEM((tall, depth), jnp.bfloat16),
            pltpu.SemaphoreType.DMA((blocks,)),
            pltpu.SemaphoreType.DMA((blocks + 1,)),
        ],
        compiler_params=pltpu.CompilerParams(vmem_limit_bytes=VMEM_MOST),
        name="pack",
    )(embeddings, pairs, live, panel)


def fill_panel(refs, columns, at, size, pan, sem):
    per_row = pan.shape[0]
    copies = []
    for ref, s in zip(refs, columns):
        for q in range(per_row):
            source = ref.at[pl.ds(at, size), pl.ds(q * BLOCK, BLOCK)]
            copies.append(
                pltpu.make_async_copy(source, pan.at[q, pl.ds(s * size, size)], sem.at[len(copies)])
            )
    for copy in copies:
        copy.start()
    return copies


def panel_of(pan, block, high):
    at = pl.ds(pl.multiple_of(block * high, high), high)
    return jnp.concatenate([pan[q, at] for q in range(pan.shape[0])], axis=0)


def add_products(pan, acc, aff, row, col):
    high = acc.shape[1] // pan.shape[0]
    forward = lax.dot_general(
        panel_of(pan, col, high), aff, (((1,), (1,)), ((), ())), preferred_element_type=jnp.float32
    )
    mirror = lax.dot_general(
        panel_of(pan, row, high), aff, (((1,), (0,)), ((), ())), preferred_element_type=jnp.float32
    )
    acc[row] += forward
    acc[col] += mirror


def write_sums(acc, joint, own, backs):
    per = own.shape[0]
    own[...] = acc[pl.ds(0, per)]
    for columns, back in zip(joint, backs):
        back[...] = sum(acc[pl.ds(s * per, per)] for s in columns).astype(jnp.bfloat16)


def pair_kernel(columns, fresh, joint, per, first, final, items, span, *refs):
    n_unit = len(columns)
    units, refs = refs[:n_unit], refs[n_unit:]
    if not first:
        acc_in, pan_in, _, refs = refs[0], refs[1], refs[2], refs[3:]
    if final:
        own, refs = refs[0], refs[1:]
        backs, refs = refs[: len(joint)], refs[len(joint) :]
        aff_out, acc, pan, refs = refs[0], refs[1], refs[2], refs[3:]
    else:
        acc, pan, aff_out, refs = refs[0], refs[1], refs[2], refs[3:]
    ubuf, affbuf, usem, psem, asem = refs
    begin, end = span[0], span[1]

    def rows_of(ref, block):
        return ref.at[pl.ds(pl.multiple_of(block * BLOCK, BLOCK), BLOCK)]

    def fetch(i, slot):
        for side in range(2):
            held = items[side, i]
            for s, ref in zip(columns, units):

                @pl.when(held // per == s)
                def _():
                    pltpu.make_async_copy(rows_of(ref, held % per), ubuf.at[slot, side], usem.at[slot, side]).start()

    def store(i, slot):
        return pltpu.make_async_copy(affbuf.at[slot], aff_out.at[i], asem.at[slot])

    @pl.when(begin < end)
    def _():
        fetch(begin, begin % 2)

    if first:
        acc[...] = jnp.zeros_like(acc)
    else:
        acc[...] = acc_in[...]
        pan[...] = pan_in[...]
    size = units[0].shape[0] - per * BLOCK - LIST_ROWS
    for copy in fill_panel(units[fresh:], columns[fresh:], per * BLOCK, size, pan, psem):
        copy.wait()

    @pl.loop(begin, end)
    def _(i):
        slot = i % 2

        @pl.when(i + 1 < end)
        def _():
            fetch(i + 1, 1 - slot)

        for side in range(2):
            pltpu.make_async_copy(rows_of(units[0], 0), ubuf.at[slot, side], usem.at[slot, side]).wait()

        @pl.when(i >= begin + 2)
        def _():
            store(i - 2, slot).wait()

        half = BLOCK // 2
        halves = []
        for part in range(2):
            scores = lax.dot_general(
                ubuf[slot, 0, pl.ds(part * half, half), :],
                ubuf[slot, 1],
                (((1,), (1,)), ((), ())),
                preferred_element_type=jnp.float32,
            )
            power = scores * (SHARPNESS * LOG2E)
            halves.append((jnp.exp2(power - 1.0) - jnp.exp2(-1.0 - power)).astype(jnp.bfloat16))
        aff = jnp.concatenate(halves, axis=0)
        affbuf[slot] = aff
        store(i, slot).start()
        add_products(pan, acc, aff, items[0, i], items[1, i])

    for back in (2, 1):

        @pl.when(end - back >= begin)
        def _():
            store(end - back, (end - back) % 2).wait()

    if final:
        write_sums(acc, joint, own, backs)


def sum_shapes(sends, per, width):
    return [jax.ShapeDtypeStruct((per, width, BLOCK), jnp.float32)] + [
        jax.ShapeDtypeStruct((per, width, BLOCK), jnp.bfloat16)
    ] * sends


def pair_call(items, span, units, columns, fresh, joint, per, width, top, state, final):
    blocks = (1 + sum(len(group) for group in joint)) * per
    depth = units[0].shape[1]
    per_row = depth // BLOCK
    smem = pl.BlockSpec(memory_space=pltpu.SMEM)
    anywhere = pl.BlockSpec(memory_space=pltpu.HBM)
    vmem = pl.BlockSpec(memory_space=pltpu.VMEM)
    operands = [items, span, *units]
    in_specs = [smem, smem] + [anywhere] * len(units)
    acc_shape = (blocks, width, BLOCK)
    pan_shape = (per_row, blocks * width // per_row, BLOCK)
    aff_shape = jax.ShapeDtypeStruct((top, BLOCK, BLOCK), jnp.bfloat16)
    scratch = [
        pltpu.VMEM((2, 2, BLOCK, depth), jnp.bfloat16),
        pltpu.VMEM((2, BLOCK, BLOCK), jnp.bfloat16),
        pltpu.SemaphoreType.DMA((2, 2)),
        pltpu.SemaphoreType.DMA((len(units) * per_row,)),
        pltpu.SemaphoreType.DMA((2,)),
    ]
    if final:
        out_shape = sum_shapes(len(joint), per, width) + [aff_shape]
        out_specs = [vmem] * (1 + len(joint)) + [anywhere]
        scratch = [pltpu.VMEM(acc_shape, jnp.float32), pltpu.VMEM(pan_shape, jnp.bfloat16)] + scratch
    else:
        out_shape = [
            jax.ShapeDtypeStruct(acc_shape, jnp.float32),
            jax.ShapeDtypeStruct(pan_shape, jnp.bfloat16),
            aff_shape,
        ]
        out_specs = [vmem, vmem, anywhere]
    aliases = {}
    if state is not None:
        aliases = {len(operands) + 2: len(out_shape) - 1}
        operands += list(state)
        in_specs += [vmem, vmem, anywhere]
    return pl.pallas_call(
        functools.partial(pair_kernel, columns, fresh, joint, per, state is None, final),
        out_shape=out_shape,
        in_specs=in_specs,
        out_specs=out_specs,
        scratch_shapes=scratch,
        input_output_aliases=aliases,
        compiler_params=pltpu.CompilerParams(vmem_limit_bytes=VMEM_LIMIT),
        name="pairs",
    )(*operands)


def apply_kernel(joint, items, span, *refs):
    n_panel = len(joint) + 1
    panels, refs = refs[:n_panel], refs[n_panel:]
    aff_in, own, backs, refs = refs[0], refs[1], refs[2 : n_panel + 1], refs[n_panel + 1 :]
    acc, pan, affbuf, psem, asem = refs
    end = span[1]

    def load(i, slot):
        return pltpu.make_async_copy(aff_in.at[i], affbuf.at[slot], asem.at[slot])

    for ahead in range(3):

        @pl.when(ahead < end)
        def _():
            load(ahead, ahead).start()

    spots = [(panels[0], 0)] + [(ref, s) for ref, group in zip(panels[1:], joint) for s in group]
    copies = fill_panel([ref for ref, _ in spots], [s for _, s in spots], 0, panels[0].shape[0], pan, psem)
    acc[...] = jnp.zeros_like(acc)
    for copy in copies:
        copy.wait()

    @pl.loop(0, end)
    def _(i):
        slot = i % 4

        @pl.when(i + 3 < end)
        def _():
            load(i + 3, (i + 3) % 4).start()

        load(i, slot).wait()
        add_products(pan, acc, affbuf[slot], items[0, i], items[1, i])

    write_sums(acc, joint, own, backs)


def apply_call(items, span, panels, joint, aff, per, width):
    held = 1 + sum(len(group) for group in joint)
    blocks = held * per
    per_row = panels[0].shape[1] // BLOCK
    smem = pl.BlockSpec(memory_space=pltpu.SMEM)
    anywhere = pl.BlockSpec(memory_space=pl.ANY)
    return pl.pallas_call(
        functools.partial(apply_kernel, joint),
        out_shape=sum_shapes(len(joint), per, width),
        in_specs=[smem, smem] + [anywhere] * len(panels) + [pl.BlockSpec(memory_space=pltpu.HBM)],
        out_specs=[pl.BlockSpec(memory_space=pltpu.VMEM)] * len(panels),
        scratch_shapes=[
            pltpu.VMEM((blocks, width, BLOCK), jnp.float32),
            pltpu.VMEM((per_row, blocks * width // per_row, BLOCK), jnp.bfloat16),
            pltpu.VMEM((4, BLOCK, BLOCK), jnp.bfloat16),
            pltpu.SemaphoreType.DMA((held * per_row,)),
            pltpu.SemaphoreType.DMA((4,)),
        ],
        compiler_params=pltpu.CompilerParams(vmem_limit_bytes=50 * 1024 * 1024),
        name="apply",
    )(items, span, *panels, aff)


def gram_kernel(n_back, own, *refs):
    backs, (y_out, gram_out) = refs[:n_back], refs[n_back:]
    gram = None
    for b in range(own.shape[0]):
        total = own[b]
        for back in backs:
            total = total + back[b].astype(jnp.float32)
        y_out[b] = total
        part = lax.dot_general(
            total,
            total,
            (((1,), (1,)), ((), ())),
            preferred_element_type=jnp.float32,
            precision=lax.Precision.HIGHEST,
        )
        gram = part if gram is None else gram + part
    gram_out[...] = gram


def gram_call(own, backs):
    width = own.shape[1]
    return pl.pallas_call(
        functools.partial(gram_kernel, len(backs)),
        out_shape=(
            jax.ShapeDtypeStruct(own.shape, jnp.float32),
            jax.ShapeDtypeStruct((width, width), jnp.float32),
        ),
        compiler_params=pltpu.CompilerParams(vmem_limit_bytes=VMEM_LIMIT),
        name="gram",
    )(own, *backs)


def inverse_factor(gram):
    width = gram.shape[0]
    row_id = lax.broadcasted_iota(jnp.int32, (width, width), 0)
    col_id = lax.broadcasted_iota(jnp.int32, (width, width), 1)
    table = jnp.concatenate([gram, (row_id == col_id).astype(jnp.float32)], axis=1)
    below = lax.broadcasted_iota(jnp.int32, (width, 1), 0)
    scale = jnp.zeros((width, 1), jnp.float32)
    for k in range(width):
        line = table[k : k + 1, :]
        pivot = table[k : k + 1, k : k + 1]
        scale = jnp.where(below == k, pivot, scale)
        factor = jnp.where(below > k, table[:, k : k + 1] / pivot, 0.0)
        table = table - factor * line
    return table[:, width:] / jnp.sqrt(scale)


def panel_kernel(rows_all, last, n_gram, *refs):
    grams, (y, out) = refs[:n_gram], refs[n_gram:]
    gram = grams[0][...]
    for other in grams[1:]:
        gram = gram + other[...]
    inverse = inverse_factor(gram * (1.0 / rows_all))
    for b in range(y.shape[0]):
        block = lax.dot_general(
            inverse,
            y[b],
            (((1,), (0,)), ((), ())),
            preferred_element_type=jnp.float32,
            precision=lax.Precision.HIGHEST,
        )
        if last:
            out[:, b * BLOCK : (b + 1) * BLOCK] = block
        else:
            per_row = out.shape[1] // BLOCK
            high = block.shape[0] // per_row
            for q in range(per_row):
                out[b * high : (b + 1) * high, q * BLOCK : (q + 1) * BLOCK] = block[
                    q * high : (q + 1) * high
                ].astype(jnp.bfloat16)


def panel_call(grams, y, rows_all, depth, last):
    blocks, width, _ = y.shape
    shape = (
        jax.ShapeDtypeStruct((width, blocks * BLOCK), jnp.float32)
        if last
        else jax.ShapeDtypeStruct((width * blocks * BLOCK // depth, depth), jnp.bfloat16)
    )
    return pl.pallas_call(
        functools.partial(panel_kernel, rows_all, last, len(grams)),
        out_shape=shape,
        compiler_params=pltpu.CompilerParams(vmem_limit_bytes=VMEM_LIMIT),
        name="panel",
    )(*grams, y)


def sum_over_rows(value):
    count = lax.axis_size("rows")
    terms, step = [value], 1
    while step < count:
        value = functools.reduce(jnp.add, terms)
        radix = min(4, count // step)
        terms = [value] + [
            lax.ppermute(value, "rows", [(i, i ^ (step * m)) for i in range(count)]) for m in range(1, radix)
        ]
        step *= radix
    return terms


def on_device(embeddings, block_pairs, pair_count, start_panel):
    count = lax.axis_size("rows")
    me = lax.axis_index("rows")
    depth = embeddings.shape[1]
    per = embeddings.shape[0] // BLOCK
    width = start_panel.shape[0]
    slots = block_pairs.shape[0]
    moves, via, hops, joint, hold, place, work, late, after, top = make_plan(count)
    held = len(moves) + 1

    merged = [functools.reduce(list.__add__, [moves[s - 1] for s in group]) for group in joint]

    def spread(value):
        got = [value]
        for group, pairs in zip(joint, merged):
            got.append(lax.ppermute(got[via.get(group[0], 0)], "rows", pairs))
        return got

    assert count * per <= 256
    own_list = jnp.concatenate([block_pairs.reshape(-1), pair_count])
    lists = {}
    for group, pairs in zip(joint, merged):
        if group[0] in late:
            part = lax.ppermute(own_list, "rows", pairs)
            lists.update({m: part for m in group})
    packed = pack_call(embeddings, block_pairs, pair_count, start_panel)
    packed, lists = lax.optimization_barrier((packed, lists))
    units = {0: packed}
    for m in range(1, len(moves) + 1):
        outgoing = units[via.get(m, 0)]
        if m in after:
            outgoing, _ = lax.optimization_barrier((outgoing, units[after[m]]))
        for pairs in hops.get(m, [moves[m - 1]]):
            outgoing = lax.ppermute(outgoing, "rows", pairs)
        units[m] = outgoing
    for m, unit in units.items():
        if m not in lists:
            lists[m] = unit[unit.shape[0] - 1, : own_list.shape[0]].astype(jnp.int32)
    lists = jnp.stack([lists[m] for m in range(held)])
    items, span_first, span_second = work_list(lists, hold, place, work, late, slots, per, top, me)
    span_all = jnp.stack([span_first[0], span_second[1]])

    early = [s for s in range(held) if s not in late]
    order = early + sorted(late)
    state = pair_call(items, span_first, [units[s] for s in early], early, 0, joint, per, width, top, None, False)
    *sums, aff = pair_call(
        items, span_second, [units[s] for s in order], order, len(early), joint, per, width, top, state, True
    )

    for sweep in range(ITERS):
        if sweep > 0:
            sums = apply_call(items, span_all, spread(panel), joint, aff, per, width)
        sums, backs = list(sums), []
        for m in sorted(range(1, len(joint) + 1), key=lambda m: m not in via):
            back = lax.ppermute(sums[m], "rows", [(target, source) for source, target in merged[m - 1]])
            if m in via:
                sums[via[m]] = sums[via[m]] + back
            else:
                backs.append(back)
        y, gram = gram_call(sums[0], backs)
        grams = sum_over_rows(gram)
        panel = panel_call(grams, y, count * embeddings.shape[0], depth, sweep == ITERS - 1)
    return panel


def solution(mesh):
    in_specs = (
        P(("groups", "rows"), None),
        P(("groups", "rows"), None),
        P(("groups", "rows")),
        P(None, ("groups", "rows")),
    )
    out_specs = P(None, ("groups", "rows"))
    return jax.shard_map(on_device, mesh=mesh, in_specs=in_specs, out_specs=out_specs, check_vma=False)
```

```python
import functools

import jax
import jax.numpy as jnp
import numpy as np
from jax import lax
from jax.experimental import pallas as pl
from jax.experimental.pallas import tpu as pltpu
from jax.sharding import PartitionSpec as P

BLOCK = 512
ITERS = 2
REACH = 7
SHARPNESS = 24.0
LOG2E = 1.4426950408889634
LIST_ROWS = 16
LANES = 128
VMEM_LIMIT = 32 * 1024 * 1024
VMEM_MOST = 55 * 1024 * 1024


def make_plan(count):
    if count == 16:
        moves = [[(i, i ^ 1) for i in range(count)], [(i, i ^ 2) for i in range(count)], [(i, i ^ 1) for i in range(count)]]
        moves.append([(i, i - 4) for i in range(4, count)])
        moves.append([(i, i + 8) for i in range(8)])
        moves.append([(i, i - 12) for i in range(12, 16)])
        late = {5, 6}
        after = {6: 4}
        via = {3: 2}
        after_back = {1: 3, 4: 3}
        hops = {5: [[(i, i + 4) for i in range(8)], [(i, i + 4) for i in range(4, 12)]]}
        joint = [[1], [2], [3], [4], [5, 6]]
    else:
        moves = [[(i, (i - o) % count) for i in range(count)] for o in range(1, REACH + 1)]
        late = {5, 6, 7}
        after = {6: 1, 7: 2}
        via = {}
        after_back = {}
        hops = {}
        joint = [[m] for m in range(1, REACH + 1)]
    hold = -np.ones((count, len(moves) + 1), np.int32)
    hold[:, 0] = np.arange(count)
    for m, pairs in enumerate(moves):
        for source, target in pairs:
            hold[target, m + 1] = hold[source, via.get(m + 1, 0)]
    work = np.zeros((count, count, count), bool)
    load = np.zeros(count, np.int32)
    for row in range(count):
        for col in range(count):
            gap = min((row - col) % count, (col - row) % count)
            if gap > REACH:
                continue
            able = [w for w in range(count) if row in hold[w] and col in hold[w]]
            pick = row if row in able else col if col in able else min(able, key=lambda w: load[w])
            work[pick, row, col] = True
            load[pick] += 1
    place = -np.ones((count, count), np.int32)
    for w in range(count):
        for s, device in enumerate(hold[w]):
            if device >= 0:
                place[w, device] = s
    return moves, via, after_back, hops, joint, hold, place, work, late, after, int(load.max())


def work_list(lists, hold, place, work, late, slots, blocks_here, top, me):
    count, held = hold.shape
    allowed = np.zeros((count, held, count), np.int32)
    for w in range(count):
        for s in range(held):
            if hold[w, s] >= 0 and place[w, hold[w, s]] == s:
                allowed[w, s] = np.where(work[w, hold[w, s]], place[w] + 1, 0)
    mine = lax.dynamic_index_in_dim(jnp.asarray(allowed), me, 0, keepdims=False)
    pairs = lists[:, : 2 * slots].reshape(held, slots, 2)
    live = jnp.arange(slots, dtype=jnp.int32)[None, :] < lists[:, 2 * slots :]
    col_owner = pairs[:, :, 1] // blocks_here
    is_col = col_owner[:, :, None] == jnp.arange(count, dtype=jnp.int32)
    col_place = jnp.sum(jnp.where(is_col, mine[:, None, :], 0), axis=2) - 1
    valid = jnp.logical_and(live, col_place >= 0)
    row_place = jnp.broadcast_to(jnp.arange(held, dtype=jnp.int32)[:, None], col_place.shape)
    is_late = functools.reduce(
        jnp.logical_or, [jnp.logical_or(row_place == s, col_place == s) for s in sorted(late)]
    )
    row_held = (row_place * blocks_here + pairs[:, :, 0] % blocks_here).reshape(-1)
    col_held = (col_place * blocks_here + pairs[:, :, 1] % blocks_here).reshape(-1)
    first = jnp.logical_and(valid, jnp.logical_not(is_late)).reshape(-1).astype(jnp.int32)
    second = jnp.logical_and(valid, is_late).reshape(-1).astype(jnp.int32)
    total = first.shape[0]
    before = jnp.arange(total)[:, None] < jnp.arange(total)[None, :]
    first_rank = jnp.sum(jnp.where(before, first[:, None], 0), axis=0)
    second_rank = jnp.sum(jnp.where(before, second[:, None], 0), axis=0)
    n_first, n_second = jnp.sum(first), jnp.sum(second)
    rank = jnp.where(first > 0, first_rank, jnp.where(second > 0, n_first + second_rank, total))
    chosen = rank[None, :] == jnp.arange(top, dtype=jnp.int32)[:, None]
    rows = jnp.sum(jnp.where(chosen, row_held[None, :], 0), axis=1)
    cols = jnp.sum(jnp.where(chosen, col_held[None, :], 0), axis=1)
    zero = jnp.zeros((), jnp.int32)
    return jnp.stack([rows, cols]), jnp.stack([zero, n_first]), jnp.stack([n_first, n_first + n_second])


def extra_kernel(pairs, live, panel, out):
    depth = out.shape[1]
    per_row = depth // BLOCK
    high = panel.shape[0] // per_row
    blocks = panel.shape[1] // BLOCK
    for b in range(blocks):
        for q in range(per_row):
            out[b * high : (b + 1) * high, q * BLOCK : (q + 1) * BLOCK] = panel[
                q * high : (q + 1) * high, b * BLOCK : (b + 1) * BLOCK
            ].astype(jnp.bfloat16)
    lane = lax.broadcasted_iota(jnp.int32, (LIST_ROWS, LANES), 1)
    values = jnp.where(lane == 2 * pairs.shape[0], live[0], 0)
    for slot in range(pairs.shape[0]):
        for side in range(2):
            values = jnp.where(lane == 2 * slot + side, pairs[slot, side], values)
    out[blocks * high :, :LANES] = values.astype(jnp.float32).astype(jnp.bfloat16)
    out[blocks * high :, LANES:] = jnp.zeros((LIST_ROWS, depth - LANES), jnp.bfloat16)


def extra_call(pairs, live, panel, depth):
    smem = pl.BlockSpec(memory_space=pltpu.SMEM)
    vmem = pl.BlockSpec(memory_space=pltpu.VMEM)
    tall = panel.shape[0] * panel.shape[1] // depth + LIST_ROWS
    return pl.pallas_call(
        extra_kernel,
        out_shape=jax.ShapeDtypeStruct((tall, depth), jnp.bfloat16),
        in_specs=[smem, smem, vmem],
        out_specs=vmem,
        compiler_params=pltpu.CompilerParams(vmem_limit_bytes=VMEM_LIMIT),
        name="extra",
    )(pairs, live, panel)


def unit_kernel(rows, out, raw, buf, scale, in_sem, out_sem):
    count, depth = rows.shape
    blocks = count // BLOCK
    step = 16
    parts = [pl.ds(b * BLOCK, BLOCK) for b in range(blocks)]
    loads = [pltpu.make_async_copy(rows.at[at], raw.at[at], in_sem.at[b]) for b, at in enumerate(parts)]
    stores = [pltpu.make_async_copy(buf.at[at], out.at[at], out_sem.at[b]) for b, at in enumerate(parts)]
    for load in loads:
        load.start()
    for b in range(blocks):
        loads[b].wait()

        @pl.loop(0, BLOCK // step, unroll=8)
        def _(i):
            values = raw[pl.ds(pl.multiple_of(b * BLOCK + i * step, step), step), :].astype(jnp.float32)
            mean = jnp.sum(values * values, axis=-1, keepdims=True) * (1.0 / depth)
            factor = lax.rsqrt(mean + 1e-06) * depth ** (-0.5)
            scale[pl.ds(pl.multiple_of(i * step, step), step), :] = jnp.broadcast_to(factor, (step, LANES))

        @pl.loop(0, BLOCK // step, unroll=8)
        def _(i):
            at = pl.ds(pl.multiple_of(b * BLOCK + i * step, step), step)
            factor = scale[pl.ds(pl.multiple_of(i * step, step), step), :]
            for lane in range(0, depth, LANES):
                values = raw[at, lane : lane + LANES].astype(jnp.float32)
                buf[at, lane : lane + LANES] = (values * factor).astype(jnp.bfloat16)

        stores[b].start()
    for store in stores:
        store.wait()


def unit_call(embeddings):
    blocks = embeddings.shape[0] // BLOCK
    return pl.pallas_call(
        unit_kernel,
        out_shape=jax.ShapeDtypeStruct(embeddings.shape, jnp.bfloat16),
        in_specs=[pl.BlockSpec(memory_space=pltpu.HBM)],
        out_specs=pl.BlockSpec(memory_space=pltpu.HBM),
        scratch_shapes=[
            pltpu.VMEM(embeddings.shape, jnp.bfloat16),
            pltpu.VMEM(embeddings.shape, jnp.bfloat16),
            pltpu.VMEM((BLOCK, LANES), jnp.float32),
            pltpu.SemaphoreType.DMA((blocks,)),
            pltpu.SemaphoreType.DMA((blocks,)),
        ],
        compiler_params=pltpu.CompilerParams(vmem_limit_bytes=VMEM_MOST),
        name="unit",
    )(embeddings)


def fill_panel(refs, joint, pan, sem):
    per_row = pan.shape[0]
    size = pan.shape[1] // (1 + sum(len(group) for group in joint))
    copies = []
    for ref, s in [(refs[0], 0)] + [(ref, s) for ref, group in zip(refs[1:], joint) for s in group]:
        for q in range(per_row):
            source = ref.at[pl.ds(0, size), pl.ds(q * BLOCK, BLOCK)]
            copies.append(
                pltpu.make_async_copy(source, pan.at[q, pl.ds(s * size, size)], sem.at[len(copies)])
            )
    for copy in copies:
        copy.start()
    return copies


def panel_of(pan, block, high):
    at = pl.ds(pl.multiple_of(block * high, high), high)
    return jnp.concatenate([pan[q, at] for q in range(pan.shape[0])], axis=0)


def add_products(pan, acc, aff, row, col):
    high = acc.shape[1] // pan.shape[0]
    forward = lax.dot_general(
        panel_of(pan, col, high), aff, (((1,), (1,)), ((), ())), preferred_element_type=jnp.float32
    )
    mirror = lax.dot_general(
        panel_of(pan, row, high), aff, (((1,), (0,)), ((), ())), preferred_element_type=jnp.float32
    )
    acc[row] += forward
    acc[col] += mirror


def write_sums(acc, joint, own, backs):
    per = own.shape[0]
    own[...] = acc[pl.ds(0, per)]
    for columns, back in zip(joint, backs):
        back[...] = sum(acc[pl.ds(s * per, per)] for s in columns).astype(jnp.bfloat16)


def pair_kernel(columns, joint, per, first, final, items, span, *refs):
    n_unit = len(columns)
    units, refs = refs[:n_unit], refs[n_unit:]
    if first:
        panels, refs = refs[: len(joint) + 1], refs[len(joint) + 1 :]
    else:
        acc_in, pan_in, _, refs = refs[0], refs[1], refs[2], refs[3:]
    if final:
        own, refs = refs[0], refs[1:]
        backs, refs = refs[: len(joint)], refs[len(joint) :]
        aff_out, acc, pan, refs = refs[0], refs[1], refs[2], refs[3:]
    else:
        acc, pan, aff_out, refs = refs[0], refs[1], refs[2], refs[3:]
    ubuf, affbuf, usem, psem, asem = refs
    begin, end = span[0], span[1]

    def rows_of(ref, block):
        return ref.at[pl.ds(pl.multiple_of(block * BLOCK, BLOCK), BLOCK)]

    def fetch(i, slot):
        for side in range(2):
            held = items[side, i]
            for s, ref in zip(columns, units):

                @pl.when(held // per == s)
                def _():
                    pltpu.make_async_copy(rows_of(ref, held % per), ubuf.at[slot, side], usem.at[slot, side]).start()

    def store(i, slot):
        return pltpu.make_async_copy(affbuf.at[slot], aff_out.at[i], asem.at[slot])

    @pl.when(begin < end)
    def _():
        fetch(begin, begin % 2)

    if first:
        copies = fill_panel(panels, joint, pan, psem)
        acc[...] = jnp.zeros_like(acc)
        for copy in copies:
            copy.wait()
    else:
        acc[...] = acc_in[...]
        pan[...] = pan_in[...]

    @pl.loop(begin, end)
    def _(i):
        slot = i % 2

        @pl.when(i + 1 < end)
        def _():
            fetch(i + 1, 1 - slot)

        for side in range(2):
            pltpu.make_async_copy(rows_of(units[0], 0), ubuf.at[slot, side], usem.at[slot, side]).wait()

        @pl.when(i >= begin + 2)
        def _():
            store(i - 2, slot).wait()

        scores = lax.dot_general(
            ubuf[slot, 0], ubuf[slot, 1], (((1,), (1,)), ((), ())), preferred_element_type=jnp.float32
        )
        power = scores * (SHARPNESS * LOG2E)
        aff = (jnp.exp2(power - 1.0) - jnp.exp2(-1.0 - power)).astype(jnp.bfloat16)
        affbuf[slot] = aff
        store(i, slot).start()
        add_products(pan, acc, aff, items[0, i], items[1, i])

    for back in (2, 1):

        @pl.when(end - back >= begin)
        def _():
            store(end - back, (end - back) % 2).wait()

    if final:
        write_sums(acc, joint, own, backs)


def sum_shapes(sends, per, width):
    return [jax.ShapeDtypeStruct((per, width, BLOCK), jnp.float32)] + [
        jax.ShapeDtypeStruct((per, width, BLOCK), jnp.bfloat16)
    ] * sends


def pair_call(items, span, units, columns, panels, joint, per, width, top, state, final):
    held = 1 + sum(len(group) for group in joint)
    blocks = held * per
    depth = units[0].shape[1]
    per_row = depth // BLOCK
    smem = pl.BlockSpec(memory_space=pltpu.SMEM)
    anywhere = pl.BlockSpec(memory_space=pltpu.HBM)
    vmem = pl.BlockSpec(memory_space=pltpu.VMEM)
    operands = [items, span, *units]
    in_specs = [smem, smem] + [anywhere] * len(units)
    acc_shape = (blocks, width, BLOCK)
    pan_shape = (per_row, blocks * width // per_row, BLOCK)
    aff_shape = jax.ShapeDtypeStruct((top, BLOCK, BLOCK), jnp.bfloat16)
    scratch = [
        pltpu.VMEM((2, 2, BLOCK, depth), jnp.bfloat16),
        pltpu.VMEM((2, BLOCK, BLOCK), jnp.bfloat16),
        pltpu.SemaphoreType.DMA((2, 2)),
        pltpu.SemaphoreType.DMA((held * per_row,)),
        pltpu.SemaphoreType.DMA((2,)),
    ]
    if final:
        out_shape = sum_shapes(len(joint), per, width) + [aff_shape]
        out_specs = [vmem] * (1 + len(joint)) + [anywhere]
        scratch = [pltpu.VMEM(acc_shape, jnp.float32), pltpu.VMEM(pan_shape, jnp.bfloat16)] + scratch
    else:
        out_shape = [
            jax.ShapeDtypeStruct(acc_shape, jnp.float32),
            jax.ShapeDtypeStruct(pan_shape, jnp.bfloat16),
            aff_shape,
        ]
        out_specs = [vmem, vmem, anywhere]
    aliases = {}
    if state is None:
        operands += panels
        in_specs += [pl.BlockSpec(memory_space=pl.ANY)] * len(panels)
    else:
        aliases = {len(operands) + 2: len(out_shape) - 1}
        operands += list(state)
        in_specs += [vmem, vmem, anywhere]
    return pl.pallas_call(
        functools.partial(pair_kernel, columns, joint, per, state is None, final),
        out_shape=out_shape,
        in_specs=in_specs,
        out_specs=out_specs,
        scratch_shapes=scratch,
        input_output_aliases=aliases,
        compiler_params=pltpu.CompilerParams(vmem_limit_bytes=VMEM_LIMIT),
        name="pairs",
    )(*operands)


def apply_kernel(joint, items, span, *refs):
    n_panel = len(joint) + 1
    panels, refs = refs[:n_panel], refs[n_panel:]
    aff_in, own, backs, refs = refs[0], refs[1], refs[2 : n_panel + 1], refs[n_panel + 1 :]
    acc, pan, affbuf, psem, asem = refs
    end = span[1]

    def load(i, slot):
        return pltpu.make_async_copy(aff_in.at[i], affbuf.at[slot], asem.at[slot])

    for ahead in range(3):

        @pl.when(ahead < end)
        def _():
            load(ahead, ahead).start()

    copies = fill_panel(panels, joint, pan, psem)
    acc[...] = jnp.zeros_like(acc)
    for copy in copies:
        copy.wait()

    @pl.loop(0, end)
    def _(i):
        slot = i % 4

        @pl.when(i + 3 < end)
        def _():
            load(i + 3, (i + 3) % 4).start()

        load(i, slot).wait()
        add_products(pan, acc, affbuf[slot], items[0, i], items[1, i])

    write_sums(acc, joint, own, backs)


def apply_call(items, span, panels, joint, aff, per, width):
    held = 1 + sum(len(group) for group in joint)
    blocks = held * per
    per_row = panels[0].shape[1] // BLOCK
    smem = pl.BlockSpec(memory_space=pltpu.SMEM)
    anywhere = pl.BlockSpec(memory_space=pl.ANY)
    return pl.pallas_call(
        functools.partial(apply_kernel, joint),
        out_shape=sum_shapes(len(joint), per, width),
        in_specs=[smem, smem] + [anywhere] * len(panels) + [pl.BlockSpec(memory_space=pltpu.HBM)],
        out_specs=[pl.BlockSpec(memory_space=pltpu.VMEM)] * len(panels),
        scratch_shapes=[
            pltpu.VMEM((blocks, width, BLOCK), jnp.float32),
            pltpu.VMEM((per_row, blocks * width // per_row, BLOCK), jnp.bfloat16),
            pltpu.VMEM((4, BLOCK, BLOCK), jnp.bfloat16),
            pltpu.SemaphoreType.DMA((held * per_row,)),
            pltpu.SemaphoreType.DMA((4,)),
        ],
        compiler_params=pltpu.CompilerParams(vmem_limit_bytes=50 * 1024 * 1024),
        name="apply",
    )(items, span, *panels, aff)


def gram_kernel(n_back, own, *refs):
    backs, (y_out, gram_out) = refs[:n_back], refs[n_back:]
    gram = None
    for b in range(own.shape[0]):
        total = own[b]
        for back in backs:
            total = total + back[b].astype(jnp.float32)
        y_out[b] = total
        part = lax.dot_general(
            total,
            total,
            (((1,), (1,)), ((), ())),
            preferred_element_type=jnp.float32,
            precision=lax.Precision.HIGHEST,
        )
        gram = part if gram is None else gram + part
    gram_out[...] = gram


def gram_call(own, backs):
    width = own.shape[1]
    return pl.pallas_call(
        functools.partial(gram_kernel, len(backs)),
        out_shape=(
            jax.ShapeDtypeStruct(own.shape, jnp.float32),
            jax.ShapeDtypeStruct((width, width), jnp.float32),
        ),
        compiler_params=pltpu.CompilerParams(vmem_limit_bytes=VMEM_LIMIT),
        name="gram",
    )(own, *backs)


def inverse_factor(gram):
    width = gram.shape[0]
    row_id = lax.broadcasted_iota(jnp.int32, (width, width), 0)
    col_id = lax.broadcasted_iota(jnp.int32, (width, width), 1)
    table = jnp.concatenate([gram, (row_id == col_id).astype(jnp.float32)], axis=1)
    tile = 8
    tiles = [table[at : at + tile] for at in range(0, width, tile)]
    shape = tiles[0].shape
    inner = lax.broadcasted_iota(jnp.int32, shape, 0)
    scales = [None] * len(tiles)
    for k in range(0, width, 2):
        home, at = k // tile, k % tile
        line0, line1 = tiles[home][at : at + 1], tiles[home][at + 1 : at + 2]
        cols0 = {g: jnp.broadcast_to(tiles[g][:, k : k + 1], shape) for g in range(home, len(tiles))}
        cols1 = {g: jnp.broadcast_to(tiles[g][:, k + 1 : k + 2], shape) for g in range(home, len(tiles))}
        a = cols0[home][at : at + 1]
        b = cols0[home][at + 1 : at + 2]
        c = cols1[home][at + 1 : at + 2]
        inv_a = 1.0 / a
        inv_s = a / (a * c - b * b)
        line1 = line1 - (b * inv_a) * line0
        line0 = inv_a * line0
        for g in range(home, len(tiles)):
            first = cols0[g] * line0
            second = ((cols1[g] - cols0[g] * (b * inv_a)) * inv_s) * line1
            if g == home:
                first = jnp.where(inner > at, first, 0.0)
                second = jnp.where(inner > at + 1, second, 0.0)
                old = scales[g] if at else jnp.zeros(shape, jnp.float32)
                scales[g] = jnp.where(inner == at, inv_a, jnp.where(inner == at + 1, inv_s, old))
            tiles[g] = tiles[g] - first - second
    return jnp.concatenate([t[:, width:] * jnp.sqrt(z[:, :width]) for t, z in zip(tiles, scales)], axis=0)


def panel_kernel(rows_all, last, n_gram, *refs):
    grams, (y, out) = refs[:n_gram], refs[n_gram:]
    gram = grams[0][...]
    for other in grams[1:]:
        gram = gram + other[...]
    inverse = inverse_factor(gram * (1.0 / rows_all))
    for b in range(y.shape[0]):
        block = lax.dot_general(
            inverse,
            y[b],
            (((1,), (0,)), ((), ())),
            preferred_element_type=jnp.float32,
            precision=lax.Precision.HIGHEST,
        )
        if last:
            out[:, b * BLOCK : (b + 1) * BLOCK] = block
        else:
            per_row = out.shape[1] // BLOCK
            high = block.shape[0] // per_row
            for q in range(per_row):
                out[b * high : (b + 1) * high, q * BLOCK : (q + 1) * BLOCK] = block[
                    q * high : (q + 1) * high
                ].astype(jnp.bfloat16)


def panel_call(grams, y, rows_all, depth, last):
    blocks, width, _ = y.shape
    shape = (
        jax.ShapeDtypeStruct((width, blocks * BLOCK), jnp.float32)
        if last
        else jax.ShapeDtypeStruct((width * blocks * BLOCK // depth, depth), jnp.bfloat16)
    )
    return pl.pallas_call(
        functools.partial(panel_kernel, rows_all, last, len(grams)),
        out_shape=shape,
        compiler_params=pltpu.CompilerParams(vmem_limit_bytes=VMEM_LIMIT),
        name="panel",
    )(*grams, y)


def sum_over_rows(value):
    count = lax.axis_size("rows")
    terms, step = [value], 1
    while step < count:
        value = functools.reduce(jnp.add, terms)
        radix = min(4, count // step)
        terms = [value] + [
            lax.ppermute(value, "rows", [(i, i ^ (step * m)) for i in range(count)]) for m in range(1, radix)
        ]
        step *= radix
    return terms


def on_device(embeddings, block_pairs, pair_count, start_panel):
    count = lax.axis_size("rows")
    me = lax.axis_index("rows")
    depth = embeddings.shape[1]
    per = embeddings.shape[0] // BLOCK
    width = start_panel.shape[0]
    slots = block_pairs.shape[0]
    moves, via, after_back, hops, joint, hold, place, work, late, after, top = make_plan(count)
    held = len(moves) + 1

    merged = [functools.reduce(list.__add__, [moves[s - 1] for s in group]) for group in joint]

    direct = [
        [(int(hold[w, s]), w) for s in group for w in range(count) if hold[w, s] >= 0] for group in joint
    ]

    def spread(value):
        got = [value]
        for group, pairs in zip(joint, merged):
            got.append(lax.ppermute(got[via.get(group[0], 0)], "rows", pairs))
        return got

    assert count * per <= 256
    extra = extra_call(block_pairs, pair_count, start_panel, depth)
    extras = [extra] + [lax.ppermute(extra, "rows", pairs) for pairs in direct]
    unit = unit_call(embeddings)
    settled, extras = lax.optimization_barrier((unit, extras))
    units = {0: unit}
    for m in range(1, len(moves) + 1):
        outgoing = units[via[m]] if m in via else unit if m in hops or m in after.values() else settled
        if m in after:
            outgoing, _ = lax.optimization_barrier((outgoing, units[after[m]]))
        for pairs in hops.get(m, [moves[m - 1]]):
            outgoing = lax.ppermute(outgoing, "rows", pairs)
        units[m] = outgoing
    lists = [part[part.shape[0] - LIST_ROWS, : 2 * slots + 1].astype(jnp.int32) for part in extras]
    lists = jnp.stack(lists[:1] + [part for part, group in zip(lists[1:], joint) for _ in group])
    items, span_first, span_second = work_list(lists, hold, place, work, late, slots, per, top, me)
    span_all = jnp.stack([span_first[0], span_second[1]])

    early = [s for s in range(held) if s not in late]
    order = early + sorted(late)
    state = pair_call(items, span_first, [units[s] for s in early], early, extras, joint, per, width, top, None, False)
    *sums, aff = pair_call(
        items, span_second, [units[s] for s in order], order, None, joint, per, width, top, state, True
    )

    for sweep in range(ITERS):
        if sweep > 0:
            sums = apply_call(items, span_all, spread(panel), joint, aff, per, width)
        sums, backs, gone = list(sums), [], {}
        for m in sorted(range(1, len(joint) + 1), key=lambda m: m not in via):
            outgoing = sums[m]
            if m in after_back:
                outgoing, _ = lax.optimization_barrier((outgoing, gone[after_back[m]]))
            back = lax.ppermute(outgoing, "rows", [(target, source) for source, target in merged[m - 1]])
            gone[m] = back
            if m in via:
                sums[via[m]] = sums[via[m]] + back
            else:
                backs.append(back)
        y, gram = gram_call(sums[0], backs)
        grams = sum_over_rows(gram)
        panel = panel_call(grams, y, count * embeddings.shape[0], depth, sweep == ITERS - 1)
    return panel


def solution(mesh):
    in_specs = (
        P(("groups", "rows"), None),
        P(("groups", "rows"), None),
        P(("groups", "rows")),
        P(None, ("groups", "rows")),
    )
    out_specs = P(None, ("groups", "rows"))
    return jax.shard_map(on_device, mesh=mesh, in_specs=in_specs, out_specs=out_specs, check_vma=False)
```

```python
import functools

import jax
import jax.numpy as jnp
import numpy as np
from jax import lax
from jax.experimental import pallas as pl
from jax.experimental.pallas import tpu as pltpu
from jax.sharding import PartitionSpec as P

BLOCK = 512
ITERS = 2
REACH = 7
SHARPNESS = 24.0
LOG2E = 1.4426950408889634
LIST_ROWS = 16
RING = 4
LANES = 128
VMEM_LIMIT = 32 * 1024 * 1024
VMEM_MOST = 55 * 1024 * 1024


def make_plan(count):
    if count == 16:
        moves = [[(i, i ^ 1) for i in range(count)], [(i, i ^ 2) for i in range(count)], [(i, i ^ 1) for i in range(count)]]
        moves.append([(i, i - 4) for i in range(4, count)])
        moves.append([(i, i + 8) for i in range(8)])
        moves.append([(i, i - 12) for i in range(12, 16)])
        late = {5, 6}
        light = {5, 6}
        after = {6: 4}
        settle = {1, 2}
        bare = True
        via = {3: 2}
        after_back = {1: 3, 4: 3}
        hops = {5: [[(i, i + 4) for i in range(8)], [(i, i + 4) for i in range(4, 12)]]}
        joint = [[1], [2], [3], [4], [5, 6]]
    else:
        moves = [[(i, (i - o) % count) for i in range(count)] for o in range(1, REACH + 1)]
        late = {5, 6, 7}
        light = late
        after = {6: 1, 7: 2}
        settle = set(range(1, REACH + 1))
        bare = False
        via = {}
        after_back = {}
        hops = {}
        joint = [[m] for m in range(1, REACH + 1)]
    hold = -np.ones((count, len(moves) + 1), np.int32)
    hold[:, 0] = np.arange(count)
    for m, pairs in enumerate(moves):
        for source, target in pairs:
            hold[target, m + 1] = hold[source, via.get(m + 1, 0)]
    work = np.zeros((count, count, count), bool)
    load = np.zeros(count, np.int32)
    for row in range(count):
        for col in range(count):
            gap = min((row - col) % count, (col - row) % count)
            if gap > REACH:
                continue
            able = [w for w in range(count) if row in hold[w] and col in hold[w]]
            pick = row if row in able else col if col in able else min(able, key=lambda w: load[w])
            work[pick, row, col] = True
            load[pick] += 1
    place = -np.ones((count, count), np.int32)
    for w in range(count):
        for s, device in enumerate(hold[w]):
            if device >= 0:
                place[w, device] = s
    return moves, via, after_back, hops, joint, hold, place, work, late, light, settle, bare, after, int(load.max())


def work_list(lists, hold, place, work, late, slots, blocks_here, top, me):
    count, held = hold.shape
    allowed = np.zeros((count, held, count), np.int32)
    for w in range(count):
        for s in range(held):
            if hold[w, s] >= 0 and place[w, hold[w, s]] == s:
                allowed[w, s] = np.where(work[w, hold[w, s]], place[w] + 1, 0)
    mine = lax.dynamic_index_in_dim(jnp.asarray(allowed), me, 0, keepdims=False)
    pairs = lists[:, : 2 * slots].reshape(held, slots, 2)
    live = jnp.arange(slots, dtype=jnp.int32)[None, :] < lists[:, 2 * slots :]
    col_owner = pairs[:, :, 1] // blocks_here
    is_col = col_owner[:, :, None] == jnp.arange(count, dtype=jnp.int32)
    col_place = jnp.sum(jnp.where(is_col, mine[:, None, :], 0), axis=2) - 1
    valid = jnp.logical_and(live, col_place >= 0)
    row_place = jnp.broadcast_to(jnp.arange(held, dtype=jnp.int32)[:, None], col_place.shape)
    is_late = functools.reduce(
        jnp.logical_or, [jnp.logical_or(row_place == s, col_place == s) for s in sorted(late)]
    )
    stage = jnp.where(valid, is_late.astype(jnp.int32), 2).reshape(-1)
    row_block, col_block = pairs[:, :, 0] % blocks_here, pairs[:, :, 1] % blocks_here
    row_held = (row_place * blocks_here + row_block).reshape(-1)
    col_held = (col_place * blocks_here + col_block).reshape(-1)
    total = stage.shape[0]
    index = jnp.arange(total, dtype=jnp.int32)
    ahead = jnp.logical_or(
        stage[:, None] < stage[None, :],
        jnp.logical_and(stage[:, None] == stage[None, :], index[:, None] < index[None, :]),
    )
    rank = jnp.where(stage < 2, jnp.sum(ahead.astype(jnp.int32), axis=0), total)
    chosen = rank[None, :] == jnp.arange(top, dtype=jnp.int32)[:, None]
    rows = jnp.sum(jnp.where(chosen, row_held[None, :], 0), axis=1)
    cols = jnp.sum(jnp.where(chosen, col_held[None, :], 0), axis=1)
    bounds = jnp.sum((stage[None, :] < jnp.arange(3, dtype=jnp.int32)[:, None]).astype(jnp.int32), axis=1)
    return jnp.stack([rows, cols]), bounds


def extra_kernel(pairs, live, panel, out):
    depth = out.shape[1]
    per_row = depth // BLOCK
    high = panel.shape[0] // per_row
    blocks = panel.shape[1] // BLOCK
    for b in range(blocks):
        for q in range(per_row):
            out[b * high : (b + 1) * high, q * BLOCK : (q + 1) * BLOCK] = panel[
                q * high : (q + 1) * high, b * BLOCK : (b + 1) * BLOCK
            ].astype(jnp.bfloat16)
    lane = lax.broadcasted_iota(jnp.int32, (LIST_ROWS, LANES), 1)
    values = jnp.where(lane == 2 * pairs.shape[1], live[0], 0)
    for slot in range(pairs.shape[1]):
        for side in range(2):
            values = jnp.where(lane == 2 * slot + side, pairs[side, slot], values)
    out[blocks * high :, :LANES] = values.astype(jnp.float32).astype(jnp.bfloat16)
    out[blocks * high :, LANES:] = jnp.zeros((LIST_ROWS, depth - LANES), jnp.bfloat16)


def extra_call(pairs, live, panel, depth):
    smem = pl.BlockSpec(memory_space=pltpu.SMEM)
    vmem = pl.BlockSpec(memory_space=pltpu.VMEM)
    tall = panel.shape[0] * panel.shape[1] // depth + LIST_ROWS
    return pl.pallas_call(
        extra_kernel,
        out_shape=jax.ShapeDtypeStruct((tall, depth), jnp.bfloat16),
        in_specs=[smem, smem, vmem],
        out_specs=vmem,
        compiler_params=pltpu.CompilerParams(vmem_limit_bytes=VMEM_LIMIT),
        name="extra",
    )(pairs, live, panel)


def pack_kernel(bare, rows, extra, *refs):
    alone, refs = refs[:bare], refs[bare:]
    out, raw, buf, scale, in_sem, alone_sem, out_sem = refs
    count, depth = rows.shape
    blocks = count // BLOCK
    step = 16
    spots = [pl.ds(b * BLOCK, BLOCK) for b in range(blocks)]
    loads = [pltpu.make_async_copy(rows.at[at], raw.at[at], in_sem.at[b]) for b, at in enumerate(spots)]
    for load in loads:
        load.start()
    tail = pltpu.make_async_copy(extra, out.at[pl.ds(count, extra.shape[0])], out_sem.at[blocks])
    tail.start()
    stores = [tail]
    for b, at in enumerate(spots):
        loads[b].wait()

        @pl.loop(0, BLOCK // step, unroll=8)
        def _(i):
            values = raw[pl.ds(pl.multiple_of(b * BLOCK + i * step, step), step), :].astype(jnp.float32)
            mean = jnp.sum(values * values, axis=-1, keepdims=True) * (1.0 / depth)
            factor = lax.rsqrt(mean + 1e-06) * depth ** (-0.5)
            scale[pl.ds(pl.multiple_of(i * step, step), step), :] = jnp.broadcast_to(factor, (step, LANES))

        @pl.loop(0, BLOCK // step, unroll=8)
        def _(i):
            here = pl.ds(pl.multiple_of(b * BLOCK + i * step, step), step)
            factor = scale[pl.ds(pl.multiple_of(i * step, step), step), :]
            for lane in range(0, depth, LANES):
                values = raw[here, lane : lane + LANES].astype(jnp.float32)
                buf[here, lane : lane + LANES] = (values * factor).astype(jnp.bfloat16)

        for ref in alone:
            stores.append(pltpu.make_async_copy(buf.at[at], ref.at[at], alone_sem.at[b]))
            stores[-1].start()
        stores.append(pltpu.make_async_copy(buf.at[at], out.at[at], out_sem.at[b]))
        stores[-1].start()
    for store in stores:
        store.wait()


def pack_call(embeddings, extra, bare):
    rows, depth = embeddings.shape
    blocks = rows // BLOCK
    hbm = pl.BlockSpec(memory_space=pltpu.HBM)
    return pl.pallas_call(
        functools.partial(pack_kernel, int(bare)),
        out_shape=[jax.ShapeDtypeStruct((rows, depth), jnp.bfloat16)] * bare
        + [jax.ShapeDtypeStruct((rows + extra.shape[0], depth), jnp.bfloat16)],
        in_specs=[hbm, pl.BlockSpec(memory_space=pltpu.VMEM)],
        out_specs=[hbm] * (bare + 1),
        scratch_shapes=[
            pltpu.VMEM((rows, depth), jnp.bfloat16),
            pltpu.VMEM((rows, depth), jnp.bfloat16),
            pltpu.VMEM((BLOCK, LANES), jnp.float32),
            pltpu.SemaphoreType.DMA((blocks,)),
            pltpu.SemaphoreType.DMA((blocks,)),
            pltpu.SemaphoreType.DMA((blocks + 1,)),
        ],
        compiler_params=pltpu.CompilerParams(vmem_limit_bytes=VMEM_MOST),
        name="pack",
    )(embeddings, extra)


def fill_panel(refs, joint, pan, sem):
    per_row = pan.shape[0]
    size = pan.shape[1] // (1 + sum(len(group) for group in joint))
    copies = []
    for ref, s in [(refs[0], 0)] + [(ref, s) for ref, group in zip(refs[1:], joint) for s in group]:
        at = max(0, ref.shape[0] - size - LIST_ROWS)
        for q in range(per_row):
            source = ref.at[pl.ds(at, size), pl.ds(q * BLOCK, BLOCK)]
            copies.append(
                pltpu.make_async_copy(source, pan.at[q, pl.ds(s * size, size)], sem.at[len(copies)])
            )
    for copy in copies:
        copy.start()
    return copies


def panel_of(pan, block, high):
    at = pl.ds(pl.multiple_of(block * high, high), high)
    return jnp.concatenate([pan[q, at] for q in range(pan.shape[0])], axis=0)


def add_products(pan, acc, aff, row, col):
    high = acc.shape[1] // pan.shape[0]
    forward = lax.dot_general(
        panel_of(pan, col, high), aff, (((1,), (1,)), ((), ())), preferred_element_type=jnp.float32
    )
    mirror = lax.dot_general(
        panel_of(pan, row, high), aff, (((1,), (0,)), ((), ())), preferred_element_type=jnp.float32
    )
    acc[row] += forward
    acc[col] += mirror


def write_sums(acc, joint, own, backs):
    per = own.shape[0]
    own[...] = acc[pl.ds(0, per)]
    for columns, back in zip(joint, backs):
        back[...] = sum(acc[pl.ds(s * per, per)] for s in columns).astype(jnp.bfloat16)


def pair_kernel(stage, held_at, n_slab, joint, per, final, items, bounds, *refs):
    n_unit = len(held_at)
    units, refs = refs[:n_unit], refs[n_unit:]
    if stage == 0:
        n_ahead = len(joint) + 1 - n_slab
        panels, refs = [*units[:n_slab], *refs[:n_ahead]], refs[n_ahead:]
        acc, pan, aff_out, refs = refs[0], refs[1], refs[2], refs[3:]
    else:
        acc_in, _, pan, refs = refs[0], refs[1], refs[2], refs[3:]
        if final:
            own, backs, refs = refs[0], refs[1 : len(joint) + 1], refs[len(joint) + 1 :]
            aff_out, acc, refs = refs[0], refs[1], refs[2:]
        else:
            acc, aff_out, refs = refs[0], refs[1], refs[2:]
    ubuf, affbuf, usem, psem, asem = refs
    begin, end = bounds[stage], bounds[stage + 1]

    def rows_of(ref, block):
        return ref.at[pl.ds(pl.multiple_of(block * BLOCK, BLOCK), BLOCK)]

    def fetch(i, slot):
        for side in range(2):
            held = items[side, i]
            for (start, size), ref in zip(held_at, units):

                @pl.when(jnp.logical_and(held >= start, held < start + size))
                def _():
                    copy = pltpu.make_async_copy(
                        rows_of(ref, held - start), ubuf.at[slot, side], usem.at[slot, side]
                    )
                    copy.start()

    def store(i, slot):
        return pltpu.make_async_copy(affbuf.at[slot], aff_out.at[i], asem.at[slot])

    for ahead in range(RING - 1):

        @pl.when(begin + ahead < end)
        def _():
            fetch(begin + ahead, (begin + ahead) % RING)

    if stage == 0:
        copies = fill_panel(panels, joint, pan, psem)
        acc[...] = jnp.zeros_like(acc)
        for copy in copies:
            copy.wait()
    else:
        acc[...] = acc_in[...]

    @pl.loop(begin, end)
    def _(i):
        slot, place = i % 2, i % RING

        @pl.when(i + RING - 1 < end)
        def _():
            fetch(i + RING - 1, (i + RING - 1) % RING)

        for side in range(2):
            pltpu.make_async_copy(rows_of(units[0], 0), ubuf.at[place, side], usem.at[place, side]).wait()

        @pl.when(i >= begin + 2)
        def _():
            store(i - 2, slot).wait()

        half = BLOCK // 2
        halves = []
        for part in range(2):
            scores = lax.dot_general(
                ubuf[place, 0],
                ubuf[place, 1, pl.ds(part * half, half), :],
                (((1,), (1,)), ((), ())),
                preferred_element_type=jnp.float32,
            )
            power = scores * (SHARPNESS * LOG2E)
            halves.append((jnp.exp2(power - 1.0) - jnp.exp2(-1.0 - power)).astype(jnp.bfloat16))
        aff = jnp.concatenate(halves, axis=1)
        affbuf[slot] = aff
        store(i, slot).start()
        add_products(pan, acc, aff, items[0, i], items[1, i])

    for back in (2, 1):

        @pl.when(end - back >= begin)
        def _():
            store(end - back, (end - back) % 2).wait()

    if final:
        write_sums(acc, joint, own, backs)


def sum_shapes(sends, per, width):
    return [jax.ShapeDtypeStruct((per, width, BLOCK), jnp.float32)] + [
        jax.ShapeDtypeStruct((per, width, BLOCK), jnp.bfloat16)
    ] * sends


def pair_call(items, bounds, stage, units, held_at, panels, state, n_slab, joint, per, width, top, final):
    held = 1 + sum(len(group) for group in joint)
    blocks = held * per
    depth = units[0].shape[1]
    per_row = depth // BLOCK
    smem = pl.BlockSpec(memory_space=pltpu.SMEM)
    hbm = pl.BlockSpec(memory_space=pltpu.HBM)
    vmem = pl.BlockSpec(memory_space=pltpu.VMEM)
    acc_shape = jax.ShapeDtypeStruct((blocks, width, BLOCK), jnp.float32)
    pan_shape = jax.ShapeDtypeStruct((per_row, blocks * width // per_row, BLOCK), jnp.bfloat16)
    aff_shape = jax.ShapeDtypeStruct((top, BLOCK, BLOCK), jnp.bfloat16)
    operands = [items, bounds, *units]
    in_specs = [smem, smem] + [hbm] * len(units)
    scratch, aliases = [], {}
    if stage == 0:
        operands += panels
        in_specs += [pl.BlockSpec(memory_space=pl.ANY)] * len(panels)
        out_shape, out_specs = [acc_shape, pan_shape, aff_shape], [vmem, vmem, hbm]
    else:
        acc, aff, pan = state
        aff_at = len(operands) + 1
        operands += [acc, aff, pan]
        in_specs += [vmem, hbm, vmem]
        if final:
            out_shape = sum_shapes(len(joint), per, width) + [aff_shape]
            out_specs = [vmem] * (1 + len(joint)) + [hbm]
            scratch = [pltpu.VMEM(acc_shape.shape, jnp.float32)]
        else:
            out_shape, out_specs = [acc_shape, aff_shape], [vmem, hbm]
        aliases = {aff_at: len(out_shape) - 1}
    return pl.pallas_call(
        functools.partial(pair_kernel, stage, held_at, n_slab, joint, per, final),
        out_shape=out_shape,
        in_specs=in_specs,
        out_specs=out_specs,
        scratch_shapes=scratch
        + [
            pltpu.VMEM((RING, 2, BLOCK, depth), jnp.bfloat16),
            pltpu.VMEM((2, BLOCK, BLOCK), jnp.bfloat16),
            pltpu.SemaphoreType.DMA((RING, 2)),
            pltpu.SemaphoreType.DMA((held * per_row,)),
            pltpu.SemaphoreType.DMA((2,)),
        ],
        input_output_aliases=aliases,
        compiler_params=pltpu.CompilerParams(vmem_limit_bytes=VMEM_LIMIT),
        name="pairs",
    )(*operands)


def apply_kernel(joint, items, bounds, *refs):
    n_panel = len(joint) + 1
    panels, refs = refs[:n_panel], refs[n_panel:]
    aff_in, own, backs, refs = refs[0], refs[1], refs[2 : n_panel + 1], refs[n_panel + 1 :]
    acc, pan, affbuf, psem, asem = refs
    end = bounds[bounds.shape[0] - 1]

    def load(i, slot):
        return pltpu.make_async_copy(aff_in.at[i], affbuf.at[slot], asem.at[slot])

    for ahead in range(3):

        @pl.when(ahead < end)
        def _():
            load(ahead, ahead).start()

    copies = fill_panel(panels, joint, pan, psem)
    acc[...] = jnp.zeros_like(acc)
    for copy in copies:
        copy.wait()

    @pl.loop(0, end)
    def _(i):
        slot = i % 4

        @pl.when(i + 3 < end)
        def _():
            load(i + 3, (i + 3) % 4).start()

        load(i, slot).wait()
        add_products(pan, acc, affbuf[slot], items[0, i], items[1, i])

    write_sums(acc, joint, own, backs)


def apply_call(items, bounds, panels, joint, aff, per, width):
    held = 1 + sum(len(group) for group in joint)
    blocks = held * per
    per_row = panels[0].shape[1] // BLOCK
    smem = pl.BlockSpec(memory_space=pltpu.SMEM)
    anywhere = pl.BlockSpec(memory_space=pl.ANY)
    return pl.pallas_call(
        functools.partial(apply_kernel, joint),
        out_shape=sum_shapes(len(joint), per, width),
        in_specs=[smem, smem] + [anywhere] * len(panels) + [pl.BlockSpec(memory_space=pltpu.HBM)],
        out_specs=[pl.BlockSpec(memory_space=pltpu.VMEM)] * len(panels),
        scratch_shapes=[
            pltpu.VMEM((blocks, width, BLOCK), jnp.float32),
            pltpu.VMEM((per_row, blocks * width // per_row, BLOCK), jnp.bfloat16),
            pltpu.VMEM((4, BLOCK, BLOCK), jnp.bfloat16),
            pltpu.SemaphoreType.DMA((held * per_row,)),
            pltpu.SemaphoreType.DMA((4,)),
        ],
        compiler_params=pltpu.CompilerParams(vmem_limit_bytes=50 * 1024 * 1024),
        name="apply",
    )(items, bounds, *panels, aff)


def gram_kernel(n_back, own, *refs):
    backs, (y_out, gram_out) = refs[:n_back], refs[n_back:]
    gram = None
    for b in range(own.shape[0]):
        total = own[b]
        for back in backs:
            total = total + back[b].astype(jnp.float32)
        y_out[b] = total
        part = lax.dot_general(
            total,
            total,
            (((1,), (1,)), ((), ())),
            preferred_element_type=jnp.float32,
            precision=lax.Precision.HIGHEST,
        )
        gram = part if gram is None else gram + part
    gram_out[...] = gram


def gram_call(own, backs):
    width = own.shape[1]
    return pl.pallas_call(
        functools.partial(gram_kernel, len(backs)),
        out_shape=(
            jax.ShapeDtypeStruct(own.shape, jnp.float32),
            jax.ShapeDtypeStruct((width, width), jnp.float32),
        ),
        compiler_params=pltpu.CompilerParams(vmem_limit_bytes=VMEM_LIMIT),
        name="gram",
    )(own, *backs)


def inverse_factor(gram):
    width = gram.shape[0]
    row_id = lax.broadcasted_iota(jnp.int32, (width, width), 0)
    col_id = lax.broadcasted_iota(jnp.int32, (width, width), 1)
    table = jnp.concatenate([gram, (row_id == col_id).astype(jnp.float32)], axis=1)
    tile = 8
    tiles = [table[at : at + tile] for at in range(0, width, tile)]
    shape = tiles[0].shape
    inner = lax.broadcasted_iota(jnp.int32, shape, 0)
    scales = [None] * len(tiles)
    for k in range(0, width, 2):
        home, at = k // tile, k % tile
        line0, line1 = tiles[home][at : at + 1], tiles[home][at + 1 : at + 2]
        cols0 = {g: jnp.broadcast_to(tiles[g][:, k : k + 1], shape) for g in range(home, len(tiles))}
        cols1 = {g: jnp.broadcast_to(tiles[g][:, k + 1 : k + 2], shape) for g in range(home, len(tiles))}
        a = cols0[home][at : at + 1]
        b = cols0[home][at + 1 : at + 2]
        c = cols1[home][at + 1 : at + 2]
        inv_a = 1.0 / a
        inv_s = a / (a * c - b * b)
        line1 = line1 - (b * inv_a) * line0
        line0 = inv_a * line0
        for g in range(home, len(tiles)):
            first = cols0[g] * line0
            second = ((cols1[g] - cols0[g] * (b * inv_a)) * inv_s) * line1
            if g == home:
                first = jnp.where(inner > at, first, 0.0)
                second = jnp.where(inner > at + 1, second, 0.0)
                old = scales[g] if at else jnp.zeros(shape, jnp.float32)
                scales[g] = jnp.where(inner == at, inv_a, jnp.where(inner == at + 1, inv_s, old))
            tiles[g] = tiles[g] - first - second
    return jnp.concatenate([t[:, width:] * jnp.sqrt(z[:, :width]) for t, z in zip(tiles, scales)], axis=0)


def panel_kernel(rows_all, last, n_gram, *refs):
    grams, (y, out) = refs[:n_gram], refs[n_gram:]
    gram = grams[0][...]
    for other in grams[1:]:
        gram = gram + other[...]
    inverse = inverse_factor(gram * (1.0 / rows_all))
    for b in range(y.shape[0]):
        block = lax.dot_general(
            inverse,
            y[b],
            (((1,), (0,)), ((), ())),
            preferred_element_type=jnp.float32,
            precision=lax.Precision.HIGHEST,
        )
        if last:
            out[:, b * BLOCK : (b + 1) * BLOCK] = block
        else:
            per_row = out.shape[1] // BLOCK
            high = block.shape[0] // per_row
            for q in range(per_row):
                out[b * high : (b + 1) * high, q * BLOCK : (q + 1) * BLOCK] = block[
                    q * high : (q + 1) * high
                ].astype(jnp.bfloat16)


def panel_call(grams, y, rows_all, depth, last):
    blocks, width, _ = y.shape
    shape = (
        jax.ShapeDtypeStruct((width, blocks * BLOCK), jnp.float32)
        if last
        else jax.ShapeDtypeStruct((width * blocks * BLOCK // depth, depth), jnp.bfloat16)
    )
    return pl.pallas_call(
        functools.partial(panel_kernel, rows_all, last, len(grams)),
        out_shape=shape,
        compiler_params=pltpu.CompilerParams(vmem_limit_bytes=VMEM_LIMIT),
        name="panel",
    )(*grams, y)


def sum_over_rows(value):
    count = lax.axis_size("rows")
    terms, step = [value], 1
    while step < count:
        value = functools.reduce(jnp.add, terms)
        radix = min(4, count // step)
        terms = [value] + [
            lax.ppermute(value, "rows", [(i, i ^ (step * m)) for i in range(count)]) for m in range(1, radix)
        ]
        step *= radix
    return terms


def on_device(embeddings, block_pairs, pair_count, start_panel):
    count = lax.axis_size("rows")
    me = lax.axis_index("rows")
    depth = embeddings.shape[1]
    per = embeddings.shape[0] // BLOCK
    width = start_panel.shape[0]
    slots = block_pairs.shape[0]
    moves, via, after_back, hops, joint, hold, place, work, late, light, settle, bare, after, top = make_plan(count)
    held = len(moves) + 1

    merged = [functools.reduce(list.__add__, [moves[s - 1] for s in group]) for group in joint]

    direct = [
        [(int(hold[w, s]), w) for s in group for w in range(count) if hold[w, s] >= 0] for group in joint
    ]

    def spread(value):
        got = [value]
        for group, pairs in zip(joint, merged):
            got.append(lax.ppermute(got[via.get(group[0], 0)], "rows", pairs))
        return got

    assert count * per <= 256
    extra = extra_call(block_pairs.T, pair_count, start_panel, depth)
    ahead = {g: lax.ppermute(extra, "rows", direct[g]) for g, group in enumerate(joint) if group[0] in light}
    *alone, packed = pack_call(embeddings, extra, bare)
    units = {0: packed}
    for m in range(1, len(moves) + 1):
        outgoing = alone[0] if m in light and bare else packed
        if m in settle:
            outgoing, ahead = lax.optimization_barrier((outgoing, ahead))
        if m in via:
            outgoing = units[via[m]]
        if m in after:
            outgoing, _ = lax.optimization_barrier((outgoing, units[after[m]]))
        for pairs in hops.get(m, [moves[m - 1]]):
            outgoing = lax.ppermute(outgoing, "rows", pairs)
        units[m] = outgoing
    early = [m for m in range(held) if m not in late]
    tails = {m: units[m] for m in early if m not in light}
    n_slab = len(tails)
    tails.update({m: ahead[g] for g in ahead for m in joint[g]})
    lists = jnp.stack(
        [tails[m][tails[m].shape[0] - LIST_ROWS, : 2 * slots + 1].astype(jnp.int32) for m in range(held)]
    )
    items, bounds = work_list(lists, hold, place, work, late, slots, per, top, me)

    order = early + sorted(late)
    held_at = [(m * per, per) for m in order]
    rows_of = [units[m] for m in order]
    shape = (n_slab, joint, per, width, top)
    n_early = len(early)
    acc, pan, aff = pair_call(
        items, bounds, 0, rows_of[:n_early], held_at[:n_early], list(ahead.values()), None, *shape, False
    )
    *sums, aff = pair_call(items, bounds, 1, rows_of, held_at, None, (acc, aff, pan), *shape, True)

    for sweep in range(ITERS):
        if sweep > 0:
            sums = apply_call(items, bounds, spread(panel), joint, aff, per, width)
        sums, backs, gone = list(sums), [], {}
        for m in sorted(range(1, len(joint) + 1), key=lambda m: m not in via):
            outgoing = sums[m]
            if m in after_back:
                outgoing, _ = lax.optimization_barrier((outgoing, gone[after_back[m]]))
            back = lax.ppermute(outgoing, "rows", [(target, source) for source, target in merged[m - 1]])
            gone[m] = back
            if m in via:
                sums[via[m]] = sums[via[m]] + back
            else:
                backs.append(back)
        y, gram = gram_call(sums[0], backs)
        grams = sum_over_rows(gram)
        panel = panel_call(grams, y, count * embeddings.shape[0], depth, sweep == ITERS - 1)
    return panel


def solution(mesh):
    in_specs = (
        P(("groups", "rows"), None),
        P(("groups", "rows"), None),
        P(("groups", "rows")),
        P(None, ("groups", "rows")),
    )
    out_specs = P(None, ("groups", "rows"))
    return jax.shard_map(on_device, mesh=mesh, in_specs=in_specs, out_specs=out_specs, check_vma=False)
```

```python
import functools

import jax
import jax.numpy as jnp
import numpy as np
from jax import lax
from jax.experimental import pallas as pl
from jax.experimental.pallas import tpu as pltpu
from jax.sharding import PartitionSpec as P

BLOCK = 512
ITERS = 2
REACH = 7
SHARPNESS = 24.0
LOG2E = 1.4426950408889634
LIST_ROWS = 16
RING = 4
LANES = 128
VMEM_LIMIT = 32 * 1024 * 1024
VMEM_MOST = 55 * 1024 * 1024


def make_plan(count):
    if count == 16:
        moves = [[(i, i ^ 1) for i in range(count)], [(i, i ^ 2) for i in range(count)], [(i, i ^ 1) for i in range(count)]]
        moves.append([(i, i - 4) for i in range(4, count)])
        moves.append([(i, i + 8) for i in range(8)])
        moves.append([(i, i - 12) for i in range(12, 16)])
        late = {5, 6}
        light = {5, 6}
        after = {6: 4}
        settle = {1, 2}
        bare = True
        via = {3: 2}
        after_back = {1: 3, 4: 3}
        hops = {5: [[(i, i + 4) for i in range(8)], [(i, i + 4) for i in range(4, 12)]]}
        joint = [[1], [2], [3], [4], [5, 6]]
    else:
        moves = [[(i, (i - o) % count) for i in range(count)] for o in range(1, REACH + 1)]
        late = {5, 6, 7}
        light = late
        after = {6: 1, 7: 2}
        settle = set(range(1, REACH + 1))
        bare = False
        via = {}
        after_back = {}
        hops = {}
        joint = [[m] for m in range(1, REACH + 1)]
    hold = -np.ones((count, len(moves) + 1), np.int32)
    hold[:, 0] = np.arange(count)
    for m, pairs in enumerate(moves):
        for source, target in pairs:
            hold[target, m + 1] = hold[source, via.get(m + 1, 0)]
    work = np.zeros((count, count, count), bool)
    load = np.zeros(count, np.int32)
    for row in range(count):
        for col in range(count):
            gap = min((row - col) % count, (col - row) % count)
            if gap > REACH:
                continue
            able = [w for w in range(count) if row in hold[w] and col in hold[w]]
            pick = row if row in able else col if col in able else min(able, key=lambda w: load[w])
            work[pick, row, col] = True
            load[pick] += 1
    place = -np.ones((count, count), np.int32)
    for w in range(count):
        for s, device in enumerate(hold[w]):
            if device >= 0:
                place[w, device] = s
    return moves, via, after_back, hops, joint, hold, place, work, late, light, settle, bare, after, int(load.max())


def work_list(lists, hold, place, work, late, slots, blocks_here, top, me):
    count, held = hold.shape
    allowed = np.zeros((count, held, count), np.int32)
    for w in range(count):
        for s in range(held):
            if hold[w, s] >= 0 and place[w, hold[w, s]] == s:
                allowed[w, s] = np.where(work[w, hold[w, s]], place[w] + 1, 0)
    mine = lax.dynamic_index_in_dim(jnp.asarray(allowed), me, 0, keepdims=False)
    pairs = lists[:, : 2 * slots].reshape(held, slots, 2)
    live = jnp.arange(slots, dtype=jnp.int32)[None, :] < lists[:, 2 * slots :]
    col_owner = pairs[:, :, 1] // blocks_here
    is_col = col_owner[:, :, None] == jnp.arange(count, dtype=jnp.int32)
    col_place = jnp.sum(jnp.where(is_col, mine[:, None, :], 0), axis=2) - 1
    valid = jnp.logical_and(live, col_place >= 0)
    row_place = jnp.broadcast_to(jnp.arange(held, dtype=jnp.int32)[:, None], col_place.shape)
    is_late = functools.reduce(
        jnp.logical_or, [jnp.logical_or(row_place == s, col_place == s) for s in sorted(late)]
    )
    stage = jnp.where(valid, is_late.astype(jnp.int32), 2).reshape(-1)
    row_block, col_block = pairs[:, :, 0] % blocks_here, pairs[:, :, 1] % blocks_here
    row_held = (row_place * blocks_here + row_block).reshape(-1)
    col_held = (col_place * blocks_here + col_block).reshape(-1)
    total = stage.shape[0]
    index = jnp.arange(total, dtype=jnp.int32)
    ahead = jnp.logical_or(
        stage[:, None] < stage[None, :],
        jnp.logical_and(stage[:, None] == stage[None, :], index[:, None] < index[None, :]),
    )
    rank = jnp.where(stage < 2, jnp.sum(ahead.astype(jnp.int32), axis=0), total)
    chosen = rank[None, :] == jnp.arange(top, dtype=jnp.int32)[:, None]
    rows = jnp.sum(jnp.where(chosen, row_held[None, :], 0), axis=1)
    cols = jnp.sum(jnp.where(chosen, col_held[None, :], 0), axis=1)
    bounds = jnp.sum((stage[None, :] < jnp.arange(3, dtype=jnp.int32)[:, None]).astype(jnp.int32), axis=1)
    return jnp.stack([rows, cols]), bounds


def extra_kernel(pairs, live, panel, out):
    depth = out.shape[1]
    per_row = depth // BLOCK
    high = panel.shape[0] // per_row
    blocks = panel.shape[1] // BLOCK
    for b in range(blocks):
        for q in range(per_row):
            out[b * high : (b + 1) * high, q * BLOCK : (q + 1) * BLOCK] = panel[
                q * high : (q + 1) * high, b * BLOCK : (b + 1) * BLOCK
            ].astype(jnp.bfloat16)
    lane = lax.broadcasted_iota(jnp.int32, (LIST_ROWS, LANES), 1)
    values = jnp.where(lane == 2 * pairs.shape[1], live[0], 0)
    for slot in range(pairs.shape[1]):
        for side in range(2):
            values = jnp.where(lane == 2 * slot + side, pairs[side, slot], values)
    out[blocks * high :, :LANES] = values.astype(jnp.float32).astype(jnp.bfloat16)
    out[blocks * high :, LANES:] = jnp.zeros((LIST_ROWS, depth - LANES), jnp.bfloat16)


def extra_call(pairs, live, panel, depth):
    smem = pl.BlockSpec(memory_space=pltpu.SMEM)
    vmem = pl.BlockSpec(memory_space=pltpu.VMEM)
    tall = panel.shape[0] * panel.shape[1] // depth + LIST_ROWS
    return pl.pallas_call(
        extra_kernel,
        out_shape=jax.ShapeDtypeStruct((tall, depth), jnp.bfloat16),
        in_specs=[smem, smem, vmem],
        out_specs=vmem,
        compiler_params=pltpu.CompilerParams(vmem_limit_bytes=VMEM_LIMIT),
        name="extra",
    )(pairs, live, panel)


def pack_kernel(bare, rows, extra, *refs):
    alone, refs = refs[:bare], refs[bare:]
    out, raw, buf, scale, in_sem, alone_sem, out_sem = refs
    count, depth = rows.shape
    blocks = count // BLOCK
    step = 16
    spots = [pl.ds(b * BLOCK, BLOCK) for b in range(blocks)]
    loads = [pltpu.make_async_copy(rows.at[at], raw.at[at], in_sem.at[b]) for b, at in enumerate(spots)]
    for load in loads:
        load.start()
    tail = pltpu.make_async_copy(extra, out.at[pl.ds(count, extra.shape[0])], out_sem.at[blocks])
    tail.start()
    stores = [tail]
    for b, at in enumerate(spots):
        loads[b].wait()

        @pl.loop(0, BLOCK // step, unroll=8)
        def _(i):
            values = raw[pl.ds(pl.multiple_of(b * BLOCK + i * step, step), step), :].astype(jnp.float32)
            mean = jnp.sum(values * values, axis=-1, keepdims=True) * (1.0 / depth)
            factor = lax.rsqrt(mean + 1e-06) * depth ** (-0.5)
            scale[pl.ds(pl.multiple_of(i * step, step), step), :] = jnp.broadcast_to(factor, (step, LANES))

        @pl.loop(0, BLOCK // step, unroll=8)
        def _(i):
            here = pl.ds(pl.multiple_of(b * BLOCK + i * step, step), step)
            factor = scale[pl.ds(pl.multiple_of(i * step, step), step), :]
            for lane in range(0, depth, LANES):
                values = raw[here, lane : lane + LANES].astype(jnp.float32)
                buf[here, lane : lane + LANES] = (values * factor).astype(jnp.bfloat16)

        for ref in alone:
            stores.append(pltpu.make_async_copy(buf.at[at], ref.at[at], alone_sem.at[b]))
            stores[-1].start()
        stores.append(pltpu.make_async_copy(buf.at[at], out.at[at], out_sem.at[b]))
        stores[-1].start()
    for store in stores:
        store.wait()


def pack_call(embeddings, extra, bare):
    rows, depth = embeddings.shape
    blocks = rows // BLOCK
    hbm = pl.BlockSpec(memory_space=pltpu.HBM)
    return pl.pallas_call(
        functools.partial(pack_kernel, int(bare)),
        out_shape=[jax.ShapeDtypeStruct((rows, depth), jnp.bfloat16)] * bare
        + [jax.ShapeDtypeStruct((rows + extra.shape[0], depth), jnp.bfloat16)],
        in_specs=[hbm, pl.BlockSpec(memory_space=pltpu.VMEM)],
        out_specs=[hbm] * (bare + 1),
        scratch_shapes=[
            pltpu.VMEM((rows, depth), jnp.bfloat16),
            pltpu.VMEM((rows, depth), jnp.bfloat16),
            pltpu.VMEM((BLOCK, LANES), jnp.float32),
            pltpu.SemaphoreType.DMA((blocks,)),
            pltpu.SemaphoreType.DMA((blocks,)),
            pltpu.SemaphoreType.DMA((blocks + 1,)),
        ],
        compiler_params=pltpu.CompilerParams(vmem_limit_bytes=VMEM_MOST),
        name="pack",
    )(embeddings, extra)


def fill_panel(refs, joint, pan, sem):
    per_row = pan.shape[0]
    size = pan.shape[1] // (1 + sum(len(group) for group in joint))
    copies = []
    for ref, s in [(refs[0], 0)] + [(ref, s) for ref, group in zip(refs[1:], joint) for s in group]:
        at = max(0, ref.shape[0] - size - LIST_ROWS)
        for q in range(per_row):
            source = ref.at[pl.ds(at, size), pl.ds(q * BLOCK, BLOCK)]
            copies.append(
                pltpu.make_async_copy(source, pan.at[q, pl.ds(s * size, size)], sem.at[len(copies)])
            )
    for copy in copies:
        copy.start()
    return copies


def panel_of(pan, block, high):
    at = pl.ds(pl.multiple_of(block * high, high), high)
    return jnp.concatenate([pan[q, at] for q in range(pan.shape[0])], axis=0)


def add_products(pan, acc, aff, row, col):
    high = acc.shape[1] // pan.shape[0]
    forward = lax.dot_general(
        panel_of(pan, col, high), aff, (((1,), (1,)), ((), ())), preferred_element_type=jnp.float32
    )
    mirror = lax.dot_general(
        panel_of(pan, row, high), aff, (((1,), (0,)), ((), ())), preferred_element_type=jnp.float32
    )
    acc[row] += forward
    acc[col] += mirror


def write_sums(acc, joint, own, backs):
    per = own.shape[0]
    own[...] = acc[pl.ds(0, per)]
    for columns, back in zip(joint, backs):
        back[...] = sum(acc[pl.ds(s * per, per)] for s in columns).astype(jnp.bfloat16)


def pair_kernel(stage, held_at, n_slab, joint, per, final, items, bounds, *refs):
    n_unit = len(held_at)
    units, refs = refs[:n_unit], refs[n_unit:]
    if stage == 0:
        n_ahead = len(joint) + 1 - n_slab
        panels, refs = [*units[:n_slab], *refs[:n_ahead]], refs[n_ahead:]
        acc, pan, aff_out, refs = refs[0], refs[1], refs[2], refs[3:]
    else:
        acc_in, _, pan, refs = refs[0], refs[1], refs[2], refs[3:]
        if final:
            own, backs, refs = refs[0], refs[1 : len(joint) + 1], refs[len(joint) + 1 :]
            aff_out, acc, refs = refs[0], refs[1], refs[2:]
        else:
            acc, aff_out, refs = refs[0], refs[1], refs[2:]
    ubuf, affbuf, usem, psem, asem = refs
    begin, end = bounds[stage], bounds[stage + 1]

    def rows_of(ref, block):
        return ref.at[pl.ds(pl.multiple_of(block * BLOCK, BLOCK), BLOCK)]

    def fetch(i, slot):
        for side in range(2):
            held = items[side, i]
            for (start, size), ref in zip(held_at, units):

                @pl.when(jnp.logical_and(held >= start, held < start + size))
                def _():
                    copy = pltpu.make_async_copy(
                        rows_of(ref, held - start), ubuf.at[slot, side], usem.at[slot, side]
                    )
                    copy.start()

    def store(i, slot):
        return pltpu.make_async_copy(affbuf.at[slot], aff_out.at[i], asem.at[slot])

    for ahead in range(RING - 1):

        @pl.when(begin + ahead < end)
        def _():
            fetch(begin + ahead, (begin + ahead) % RING)

    if stage == 0:
        copies = fill_panel(panels, joint, pan, psem)
        acc[...] = jnp.zeros_like(acc)
        for copy in copies:
            copy.wait()
    else:
        acc[...] = acc_in[...]

    @pl.loop(begin, end)
    def _(i):
        slot, place = i % 2, i % RING

        @pl.when(i + RING - 1 < end)
        def _():
            fetch(i + RING - 1, (i + RING - 1) % RING)

        for side in range(2):
            pltpu.make_async_copy(rows_of(units[0], 0), ubuf.at[place, side], usem.at[place, side]).wait()

        @pl.when(i >= begin + 2)
        def _():
            store(i - 2, slot).wait()

        half = BLOCK // 2
        halves = []
        for part in range(2):
            scores = lax.dot_general(
                ubuf[place, 0],
                ubuf[place, 1, pl.ds(part * half, half), :],
                (((1,), (1,)), ((), ())),
                preferred_element_type=jnp.float32,
            )
            power = scores * (SHARPNESS * LOG2E)
            halves.append((jnp.exp2(power - 1.0) - jnp.exp2(-1.0 - power)).astype(jnp.bfloat16))
        aff = jnp.concatenate(halves, axis=1)
        affbuf[slot] = aff
        store(i, slot).start()
        add_products(pan, acc, aff, items[0, i], items[1, i])

    for back in (2, 1):

        @pl.when(end - back >= begin)
        def _():
            store(end - back, (end - back) % 2).wait()

    if final:
        write_sums(acc, joint, own, backs)


def sum_shapes(sends, per, width):
    return [jax.ShapeDtypeStruct((per, width, BLOCK), jnp.float32)] + [
        jax.ShapeDtypeStruct((per, width, BLOCK), jnp.bfloat16)
    ] * sends


def pair_call(items, bounds, stage, units, held_at, panels, state, n_slab, joint, per, width, top, final):
    held = 1 + sum(len(group) for group in joint)
    blocks = held * per
    depth = units[0].shape[1]
    per_row = depth // BLOCK
    smem = pl.BlockSpec(memory_space=pltpu.SMEM)
    hbm = pl.BlockSpec(memory_space=pltpu.HBM)
    vmem = pl.BlockSpec(memory_space=pltpu.VMEM)
    acc_shape = jax.ShapeDtypeStruct((blocks, width, BLOCK), jnp.float32)
    pan_shape = jax.ShapeDtypeStruct((per_row, blocks * width // per_row, BLOCK), jnp.bfloat16)
    aff_shape = jax.ShapeDtypeStruct((top, BLOCK, BLOCK), jnp.bfloat16)
    operands = [items, bounds, *units]
    in_specs = [smem, smem] + [hbm] * len(units)
    scratch, aliases = [], {}
    if stage == 0:
        operands += panels
        in_specs += [pl.BlockSpec(memory_space=pl.ANY)] * len(panels)
        out_shape, out_specs = [acc_shape, pan_shape, aff_shape], [vmem, vmem, hbm]
    else:
        acc, aff, pan = state
        aff_at = len(operands) + 1
        operands += [acc, aff, pan]
        in_specs += [vmem, hbm, vmem]
        if final:
            out_shape = sum_shapes(len(joint), per, width) + [aff_shape]
            out_specs = [vmem] * (1 + len(joint)) + [hbm]
            scratch = [pltpu.VMEM(acc_shape.shape, jnp.float32)]
        else:
            out_shape, out_specs = [acc_shape, aff_shape], [vmem, hbm]
        aliases = {aff_at: len(out_shape) - 1}
    return pl.pallas_call(
        functools.partial(pair_kernel, stage, held_at, n_slab, joint, per, final),
        out_shape=out_shape,
        in_specs=in_specs,
        out_specs=out_specs,
        scratch_shapes=scratch
        + [
            pltpu.VMEM((RING, 2, BLOCK, depth), jnp.bfloat16),
            pltpu.VMEM((2, BLOCK, BLOCK), jnp.bfloat16),
            pltpu.SemaphoreType.DMA((RING, 2)),
            pltpu.SemaphoreType.DMA((held * per_row,)),
            pltpu.SemaphoreType.DMA((2,)),
        ],
        input_output_aliases=aliases,
        compiler_params=pltpu.CompilerParams(vmem_limit_bytes=VMEM_LIMIT),
        name="pairs",
    )(*operands)


def apply_kernel(joint, items, bounds, *refs):
    n_panel = len(joint) + 1
    panels, refs = refs[:n_panel], refs[n_panel:]
    aff_in, own, backs, refs = refs[0], refs[1], refs[2 : n_panel + 1], refs[n_panel + 1 :]
    acc, pan, affbuf, psem, asem = refs
    end = bounds[bounds.shape[0] - 1]

    def load(i, slot):
        return pltpu.make_async_copy(aff_in.at[i], affbuf.at[slot], asem.at[slot])

    for ahead in range(3):

        @pl.when(ahead < end)
        def _():
            load(ahead, ahead).start()

    copies = fill_panel(panels, joint, pan, psem)
    acc[...] = jnp.zeros_like(acc)
    for copy in copies:
        copy.wait()

    @pl.loop(0, end)
    def _(i):
        slot = i % 4

        @pl.when(i + 3 < end)
        def _():
            load(i + 3, (i + 3) % 4).start()

        load(i, slot).wait()
        add_products(pan, acc, affbuf[slot], items[0, i], items[1, i])

    write_sums(acc, joint, own, backs)


def apply_call(items, bounds, panels, joint, aff, per, width):
    held = 1 + sum(len(group) for group in joint)
    blocks = held * per
    per_row = panels[0].shape[1] // BLOCK
    smem = pl.BlockSpec(memory_space=pltpu.SMEM)
    anywhere = pl.BlockSpec(memory_space=pl.ANY)
    return pl.pallas_call(
        functools.partial(apply_kernel, joint),
        out_shape=sum_shapes(len(joint), per, width),
        in_specs=[smem, smem] + [anywhere] * len(panels) + [pl.BlockSpec(memory_space=pltpu.HBM)],
        out_specs=[pl.BlockSpec(memory_space=pltpu.VMEM)] * len(panels),
        scratch_shapes=[
            pltpu.VMEM((blocks, width, BLOCK), jnp.float32),
            pltpu.VMEM((per_row, blocks * width // per_row, BLOCK), jnp.bfloat16),
            pltpu.VMEM((4, BLOCK, BLOCK), jnp.bfloat16),
            pltpu.SemaphoreType.DMA((held * per_row,)),
            pltpu.SemaphoreType.DMA((4,)),
        ],
        compiler_params=pltpu.CompilerParams(vmem_limit_bytes=50 * 1024 * 1024),
        name="apply",
    )(items, bounds, *panels, aff)


def gram_kernel(n_back, own, *refs):
    backs, (y_out, gram_out) = refs[:n_back], refs[n_back:]
    gram = None
    for b in range(own.shape[0]):
        total = own[b]
        for back in backs:
            total = total + back[b].astype(jnp.float32)
        y_out[b] = total
        part = lax.dot_general(
            total,
            total,
            (((1,), (1,)), ((), ())),
            preferred_element_type=jnp.float32,
            precision=lax.Precision.HIGHEST,
        )
        gram = part if gram is None else gram + part
    gram_out[...] = gram


def gram_call(own, backs):
    width = own.shape[1]
    return pl.pallas_call(
        functools.partial(gram_kernel, len(backs)),
        out_shape=(
            jax.ShapeDtypeStruct(own.shape, jnp.float32),
            jax.ShapeDtypeStruct((width, width), jnp.float32),
        ),
        compiler_params=pltpu.CompilerParams(vmem_limit_bytes=VMEM_LIMIT),
        name="gram",
    )(own, *backs)


def inverse_factor(gram):
    width = gram.shape[0]
    row_id = lax.broadcasted_iota(jnp.int32, (width, width), 0)
    col_id = lax.broadcasted_iota(jnp.int32, (width, width), 1)
    table = jnp.concatenate([gram, (row_id == col_id).astype(jnp.float32)], axis=1)
    tile = 8
    tiles = [table[at : at + tile] for at in range(0, width, tile)]
    shape = tiles[0].shape
    inner = lax.broadcasted_iota(jnp.int32, shape, 0)
    scales = [None] * len(tiles)
    for k in range(0, width, 2):
        home, at = k // tile, k % tile
        line0, line1 = tiles[home][at : at + 1], tiles[home][at + 1 : at + 2]
        cols0 = {g: jnp.broadcast_to(tiles[g][:, k : k + 1], shape) for g in range(home, len(tiles))}
        cols1 = {g: jnp.broadcast_to(tiles[g][:, k + 1 : k + 2], shape) for g in range(home, len(tiles))}
        a = cols0[home][at : at + 1]
        b = cols0[home][at + 1 : at + 2]
        c = cols1[home][at + 1 : at + 2]
        inv_a = 1.0 / a
        inv_s = a / (a * c - b * b)
        line1 = line1 - (b * inv_a) * line0
        line0 = inv_a * line0
        for g in range(home, len(tiles)):
            first = cols0[g] * line0
            second = ((cols1[g] - cols0[g] * (b * inv_a)) * inv_s) * line1
            if g == home:
                first = jnp.where(inner > at, first, 0.0)
                second = jnp.where(inner > at + 1, second, 0.0)
                old = scales[g] if at else jnp.zeros(shape, jnp.float32)
                scales[g] = jnp.where(inner == at, inv_a, jnp.where(inner == at + 1, inv_s, old))
            tiles[g] = tiles[g] - first - second
    return jnp.concatenate([t[:, width:] * jnp.sqrt(z[:, :width]) for t, z in zip(tiles, scales)], axis=0)


def panel_kernel(rows_all, last, n_gram, *refs):
    grams, (y, out) = refs[:n_gram], refs[n_gram:]
    gram = grams[0][...]
    for other in grams[1:]:
        gram = gram + other[...]
    inverse = inverse_factor(gram * (1.0 / rows_all))
    for b in range(y.shape[0]):
        block = lax.dot_general(
            inverse,
            y[b],
            (((1,), (0,)), ((), ())),
            preferred_element_type=jnp.float32,
            precision=lax.Precision.HIGHEST,
        )
        if last:
            out[:, b * BLOCK : (b + 1) * BLOCK] = block
        else:
            per_row = out.shape[1] // BLOCK
            high = block.shape[0] // per_row
            for q in range(per_row):
                out[b * high : (b + 1) * high, q * BLOCK : (q + 1) * BLOCK] = block[
                    q * high : (q + 1) * high
                ].astype(jnp.bfloat16)


def panel_call(grams, y, rows_all, depth, last):
    blocks, width, _ = y.shape
    shape = (
        jax.ShapeDtypeStruct((width, blocks * BLOCK), jnp.float32)
        if last
        else jax.ShapeDtypeStruct((width * blocks * BLOCK // depth, depth), jnp.bfloat16)
    )
    return pl.pallas_call(
        functools.partial(panel_kernel, rows_all, last, len(grams)),
        out_shape=shape,
        compiler_params=pltpu.CompilerParams(vmem_limit_bytes=VMEM_LIMIT),
        name="panel",
    )(*grams, y)


def sum_over_rows(value):
    count = lax.axis_size("rows")
    rounds, step = [], 1
    while step < count:
        radix = min(4, count // step)
        rounds.append((step, radix))
        step *= radix
    terms = [value]
    for step, radix in reversed(rounds):
        value = functools.reduce(jnp.add, terms)
        terms = [value] + [
            lax.ppermute(value, "rows", [(i, i ^ (step * m)) for i in range(count)]) for m in range(1, radix)
        ]
    return terms


def on_device(embeddings, block_pairs, pair_count, start_panel):
    count = lax.axis_size("rows")
    me = lax.axis_index("rows")
    depth = embeddings.shape[1]
    per = embeddings.shape[0] // BLOCK
    width = start_panel.shape[0]
    slots = block_pairs.shape[0]
    moves, via, after_back, hops, joint, hold, place, work, late, light, settle, bare, after, top = make_plan(count)
    held = len(moves) + 1

    merged = [functools.reduce(list.__add__, [moves[s - 1] for s in group]) for group in joint]

    direct = [
        [(int(hold[w, s]), w) for s in group for w in range(count) if hold[w, s] >= 0] for group in joint
    ]

    def spread(value):
        got = {0: value}
        for n in sorted(range(1, len(joint) + 1), key=lambda n: n in after_back):
            outgoing = got[via.get(joint[n - 1][0], 0)]
            if n in after_back:
                outgoing, _ = lax.optimization_barrier((outgoing, got[via[after_back[n]]]))
            got[n] = lax.ppermute(outgoing, "rows", merged[n - 1])
        return [got[n] for n in range(len(joint) + 1)]

    assert count * per <= 256
    extra = extra_call(block_pairs.T, pair_count, start_panel, depth)
    ahead = {g: lax.ppermute(extra, "rows", direct[g]) for g, group in enumerate(joint) if group[0] in light}
    *alone, packed = pack_call(embeddings, extra, bare)
    units = {0: packed}
    for m in range(1, len(moves) + 1):
        outgoing = alone[0] if m in light and bare else packed
        if m in settle:
            outgoing, ahead = lax.optimization_barrier((outgoing, ahead))
        if m in via:
            outgoing = units[via[m]]
        if m in after:
            outgoing, _ = lax.optimization_barrier((outgoing, units[after[m]]))
        for pairs in hops.get(m, [moves[m - 1]]):
            outgoing = lax.ppermute(outgoing, "rows", pairs)
        units[m] = outgoing
    early = [m for m in range(held) if m not in late]
    tails = {m: units[m] for m in early if m not in light}
    n_slab = len(tails)
    tails.update({m: ahead[g] for g in ahead for m in joint[g]})
    lists = jnp.stack(
        [tails[m][tails[m].shape[0] - LIST_ROWS, : 2 * slots + 1].astype(jnp.int32) for m in range(held)]
    )
    items, bounds = work_list(lists, hold, place, work, late, slots, per, top, me)

    order = early + sorted(late)
    held_at = [(m * per, per) for m in order]
    rows_of = [units[m] for m in order]
    shape = (n_slab, joint, per, width, top)
    n_early = len(early)
    acc, pan, aff = pair_call(
        items, bounds, 0, rows_of[:n_early], held_at[:n_early], list(ahead.values()), None, *shape, False
    )
    *sums, aff = pair_call(items, bounds, 1, rows_of, held_at, None, (acc, aff, pan), *shape, True)

    for sweep in range(ITERS):
        if sweep > 0:
            sums = apply_call(items, bounds, spread(panel), joint, aff, per, width)
        sums, backs, gone = list(sums), [], {}
        for m in sorted(range(1, len(joint) + 1), key=lambda m: m not in via):
            outgoing = sums[m]
            if m in after_back:
                outgoing, _ = lax.optimization_barrier((outgoing, gone[after_back[m]]))
            back = lax.ppermute(outgoing, "rows", [(target, source) for source, target in merged[m - 1]])
            gone[m] = back
            if m in via:
                sums[via[m]] = sums[via[m]] + back
            else:
                backs.append(back)
        y, gram = gram_call(sums[0], backs)
        grams = sum_over_rows(gram)
        panel = panel_call(grams, y, count * embeddings.shape[0], depth, sweep == ITERS - 1)
    return panel


def solution(mesh):
    in_specs = (
        P(("groups", "rows"), None),
        P(("groups", "rows"), None),
        P(("groups", "rows")),
        P(None, ("groups", "rows")),
    )
    out_specs = P(None, ("groups", "rows"))
    return jax.shard_map(on_device, mesh=mesh, in_specs=in_specs, out_specs=out_specs, check_vma=False)
```

```python
import functools

import jax
import jax.numpy as jnp
import numpy as np
from jax import lax
from jax.experimental import pallas as pl
from jax.experimental.pallas import tpu as pltpu
from jax.sharding import PartitionSpec as P

BLOCK = 512
ITERS = 2
REACH = 7
SHARPNESS = 24.0
LOG2E = 1.4426950408889634
LIST_ROWS = 16
RING = 4
APPLY_RING = 8
LANES = 128
VMEM_LIMIT = 32 * 1024 * 1024
VMEM_MOST = 55 * 1024 * 1024


def make_plan(count):
    if count == 16:
        moves = [[(i, i ^ 1) for i in range(count)], [(i, i ^ 2) for i in range(count)], [(i, i ^ 1) for i in range(count)]]
        moves.append([(i, i - 4) for i in range(4, count)])
        moves.append([(i, i + 8) for i in range(8)])
        moves.append([(i, i - 12) for i in range(12, 16)])
        late = {5, 6}
        light = {5, 6}
        after = {6: 4}
        settle = {1, 2}
        bare = True
        via = {3: 2}
        after_back = {1: 3, 4: 3}
        hops = {5: [[(i, i + 4) for i in range(8)], [(i, i + 4) for i in range(4, 12)]]}
        joint = [[1], [2], [3], [4], [5, 6]]
    else:
        moves = [[(i, (i - o) % count) for i in range(count)] for o in range(1, REACH + 1)]
        late = {5, 6, 7}
        light = late
        after = {6: 1, 7: 2}
        settle = set(range(1, REACH + 1))
        bare = False
        via = {}
        after_back = {}
        hops = {}
        joint = [[m] for m in range(1, REACH + 1)]
    hold = -np.ones((count, len(moves) + 1), np.int32)
    hold[:, 0] = np.arange(count)
    for m, pairs in enumerate(moves):
        for source, target in pairs:
            hold[target, m + 1] = hold[source, via.get(m + 1, 0)]
    work = np.zeros((count, count, count), bool)
    load = np.zeros(count, np.int32)
    for row in range(count):
        for col in range(count):
            gap = min((row - col) % count, (col - row) % count)
            if gap > REACH:
                continue
            able = [w for w in range(count) if row in hold[w] and col in hold[w]]
            pick = row if row in able else col if col in able else min(able, key=lambda w: load[w])
            work[pick, row, col] = True
            load[pick] += 1
    place = -np.ones((count, count), np.int32)
    for w in range(count):
        for s, device in enumerate(hold[w]):
            if device >= 0:
                place[w, device] = s
    return moves, via, after_back, hops, joint, hold, place, work, late, light, settle, bare, after, int(load.max())


def work_list(lists, hold, place, work, late, slots, blocks_here, top, me):
    count, held = hold.shape
    allowed = np.zeros((count, held, count), np.int32)
    for w in range(count):
        for s in range(held):
            if hold[w, s] >= 0 and place[w, hold[w, s]] == s:
                allowed[w, s] = np.where(work[w, hold[w, s]], place[w] + 1, 0)
    mine = lax.dynamic_index_in_dim(jnp.asarray(allowed), me, 0, keepdims=False)
    pairs = lists[:, : 2 * slots].reshape(held, slots, 2)
    live = jnp.arange(slots, dtype=jnp.int32)[None, :] < lists[:, 2 * slots :]
    col_owner = pairs[:, :, 1] // blocks_here
    is_col = col_owner[:, :, None] == jnp.arange(count, dtype=jnp.int32)
    col_place = jnp.sum(jnp.where(is_col, mine[:, None, :], 0), axis=2) - 1
    valid = jnp.logical_and(live, col_place >= 0)
    row_place = jnp.broadcast_to(jnp.arange(held, dtype=jnp.int32)[:, None], col_place.shape)
    is_late = functools.reduce(
        jnp.logical_or, [jnp.logical_or(row_place == s, col_place == s) for s in sorted(late)]
    )
    stage = jnp.where(valid, is_late.astype(jnp.int32), 2).reshape(-1)
    row_block, col_block = pairs[:, :, 0] % blocks_here, pairs[:, :, 1] % blocks_here
    row_held = (row_place * blocks_here + row_block).reshape(-1)
    col_held = (col_place * blocks_here + col_block).reshape(-1)
    total = stage.shape[0]
    index = jnp.arange(total, dtype=jnp.int32)
    ahead = jnp.logical_or(
        stage[:, None] < stage[None, :],
        jnp.logical_and(stage[:, None] == stage[None, :], index[:, None] < index[None, :]),
    )
    rank = jnp.where(stage < 2, jnp.sum(ahead.astype(jnp.int32), axis=0), total)
    chosen = rank[None, :] == jnp.arange(top, dtype=jnp.int32)[:, None]
    rows = jnp.sum(jnp.where(chosen, row_held[None, :], 0), axis=1)
    cols = jnp.sum(jnp.where(chosen, col_held[None, :], 0), axis=1)
    bounds = jnp.sum((stage[None, :] < jnp.arange(3, dtype=jnp.int32)[:, None]).astype(jnp.int32), axis=1)
    return jnp.stack([rows, cols]), bounds


def extra_kernel(pairs, live, panel, out):
    depth = out.shape[1]
    per_row = depth // BLOCK
    high = panel.shape[0] // per_row
    blocks = panel.shape[1] // BLOCK
    for b in range(blocks):
        for q in range(per_row):
            out[b * high : (b + 1) * high, q * BLOCK : (q + 1) * BLOCK] = panel[
                q * high : (q + 1) * high, b * BLOCK : (b + 1) * BLOCK
            ].astype(jnp.bfloat16)
    lane = lax.broadcasted_iota(jnp.int32, (LIST_ROWS, LANES), 1)
    values = jnp.where(lane == 2 * pairs.shape[1], live[0], 0)
    for slot in range(pairs.shape[1]):
        for side in range(2):
            values = jnp.where(lane == 2 * slot + side, pairs[side, slot], values)
    out[blocks * high :, :LANES] = values.astype(jnp.float32).astype(jnp.bfloat16)
    out[blocks * high :, LANES:] = jnp.zeros((LIST_ROWS, depth - LANES), jnp.bfloat16)


def extra_call(pairs, live, panel, depth):
    smem = pl.BlockSpec(memory_space=pltpu.SMEM)
    vmem = pl.BlockSpec(memory_space=pltpu.VMEM)
    tall = panel.shape[0] * panel.shape[1] // depth + LIST_ROWS
    return pl.pallas_call(
        extra_kernel,
        out_shape=jax.ShapeDtypeStruct((tall, depth), jnp.bfloat16),
        in_specs=[smem, smem, vmem],
        out_specs=vmem,
        compiler_params=pltpu.CompilerParams(vmem_limit_bytes=VMEM_LIMIT),
        name="extra",
    )(pairs, live, panel)


def pack_kernel(bare, rows, extra, *refs):
    alone, refs = refs[:bare], refs[bare:]
    out, raw, buf, scale, in_sem, alone_sem, out_sem = refs
    count, depth = rows.shape
    blocks = count // BLOCK
    step = 16
    spots = [pl.ds(b * BLOCK, BLOCK) for b in range(blocks)]
    loads = [pltpu.make_async_copy(rows.at[at], raw.at[at], in_sem.at[b]) for b, at in enumerate(spots)]
    for load in loads:
        load.start()
    tail = pltpu.make_async_copy(extra, out.at[pl.ds(count, extra.shape[0])], out_sem.at[blocks])
    tail.start()
    stores = [tail]
    for b, at in enumerate(spots):
        loads[b].wait()

        @pl.loop(0, BLOCK // step, unroll=8)
        def _(i):
            values = raw[pl.ds(pl.multiple_of(b * BLOCK + i * step, step), step), :].astype(jnp.float32)
            mean = jnp.sum(values * values, axis=-1, keepdims=True) * (1.0 / depth)
            factor = lax.rsqrt(mean + 1e-06) * depth ** (-0.5)
            scale[pl.ds(pl.multiple_of(i * step, step), step), :] = jnp.broadcast_to(factor, (step, LANES))

        @pl.loop(0, BLOCK // step, unroll=8)
        def _(i):
            here = pl.ds(pl.multiple_of(b * BLOCK + i * step, step), step)
            factor = scale[pl.ds(pl.multiple_of(i * step, step), step), :]
            for lane in range(0, depth, LANES):
                values = raw[here, lane : lane + LANES].astype(jnp.float32)
                buf[here, lane : lane + LANES] = (values * factor).astype(jnp.bfloat16)

        for ref in alone:
            stores.append(pltpu.make_async_copy(buf.at[at], ref.at[at], alone_sem.at[b]))
            stores[-1].start()
        stores.append(pltpu.make_async_copy(buf.at[at], out.at[at], out_sem.at[b]))
        stores[-1].start()
    for store in stores:
        store.wait()


def pack_call(embeddings, extra, bare):
    rows, depth = embeddings.shape
    blocks = rows // BLOCK
    hbm = pl.BlockSpec(memory_space=pltpu.HBM)
    return pl.pallas_call(
        functools.partial(pack_kernel, int(bare)),
        out_shape=[jax.ShapeDtypeStruct((rows, depth), jnp.bfloat16)] * bare
        + [jax.ShapeDtypeStruct((rows + extra.shape[0], depth), jnp.bfloat16)],
        in_specs=[hbm, pl.BlockSpec(memory_space=pltpu.VMEM)],
        out_specs=[hbm] * (bare + 1),
        scratch_shapes=[
            pltpu.VMEM((rows, depth), jnp.bfloat16),
            pltpu.VMEM((rows, depth), jnp.bfloat16),
            pltpu.VMEM((BLOCK, LANES), jnp.float32),
            pltpu.SemaphoreType.DMA((blocks,)),
            pltpu.SemaphoreType.DMA((blocks,)),
            pltpu.SemaphoreType.DMA((blocks + 1,)),
        ],
        compiler_params=pltpu.CompilerParams(vmem_limit_bytes=VMEM_MOST),
        name="pack",
    )(embeddings, extra)


def fill_panel(refs, joint, pan, sem):
    per_row = pan.shape[0]
    size = pan.shape[1] // (1 + sum(len(group) for group in joint))
    copies = []
    for ref, s in [(refs[0], 0)] + [(ref, s) for ref, group in zip(refs[1:], joint) for s in group]:
        at = max(0, ref.shape[0] - size - LIST_ROWS)
        for q in range(per_row):
            source = ref.at[pl.ds(at, size), pl.ds(q * BLOCK, BLOCK)]
            copies.append(
                pltpu.make_async_copy(source, pan.at[q, pl.ds(s * size, size)], sem.at[len(copies)])
            )
    for copy in copies:
        copy.start()
    return copies


def panel_of(pan, block, high):
    at = pl.ds(pl.multiple_of(block * high, high), high)
    return jnp.concatenate([pan[q, at] for q in range(pan.shape[0])], axis=0)


def add_products(pan, acc, aff, row, col):
    high = acc.shape[1] // pan.shape[0]
    forward = lax.dot_general(
        panel_of(pan, col, high), aff, (((1,), (1,)), ((), ())), preferred_element_type=jnp.float32
    )
    mirror = lax.dot_general(
        panel_of(pan, row, high), aff, (((1,), (0,)), ((), ())), preferred_element_type=jnp.float32
    )
    acc[row] += forward
    acc[col] += mirror


def write_sums(acc, joint, own, backs):
    per = own.shape[0]
    own[...] = acc[pl.ds(0, per)]
    for columns, back in zip(joint, backs):
        back[...] = sum(acc[pl.ds(s * per, per)] for s in columns).astype(jnp.bfloat16)


def pair_kernel(stage, held_at, n_slab, joint, per, final, items, bounds, *refs):
    n_unit = len(held_at)
    units, refs = refs[:n_unit], refs[n_unit:]
    if stage == 0:
        n_ahead = len(joint) + 1 - n_slab
        panels, refs = [*units[:n_slab], *refs[:n_ahead]], refs[n_ahead:]
        acc, pan, aff_out, refs = refs[0], refs[1], refs[2], refs[3:]
    else:
        acc_in, _, pan, refs = refs[0], refs[1], refs[2], refs[3:]
        if final:
            own, backs, refs = refs[0], refs[1 : len(joint) + 1], refs[len(joint) + 1 :]
            aff_out, acc, refs = refs[0], refs[1], refs[2:]
        else:
            acc, aff_out, refs = refs[0], refs[1], refs[2:]
    ubuf, affbuf, usem, psem, asem = refs
    begin, end = bounds[stage], bounds[stage + 1]

    def rows_of(ref, block):
        return ref.at[pl.ds(pl.multiple_of(block * BLOCK, BLOCK), BLOCK)]

    def fetch(i, slot):
        for side in range(2):
            held = items[side, i]
            for (start, size), ref in zip(held_at, units):

                @pl.when(jnp.logical_and(held >= start, held < start + size))
                def _():
                    copy = pltpu.make_async_copy(
                        rows_of(ref, held - start), ubuf.at[slot, side], usem.at[slot, side]
                    )
                    copy.start()

    def store(i, slot):
        return pltpu.make_async_copy(affbuf.at[slot], aff_out.at[i], asem.at[slot])

    for ahead in range(RING - 1):

        @pl.when(begin + ahead < end)
        def _():
            fetch(begin + ahead, (begin + ahead) % RING)

    if stage == 0:
        copies = fill_panel(panels, joint, pan, psem)
        acc[...] = jnp.zeros_like(acc)
        for copy in copies:
            copy.wait()
    else:
        acc[...] = acc_in[...]

    @pl.loop(begin, end)
    def _(i):
        slot, place = i % 2, i % RING

        @pl.when(i + RING - 1 < end)
        def _():
            fetch(i + RING - 1, (i + RING - 1) % RING)

        for side in range(2):
            pltpu.make_async_copy(rows_of(units[0], 0), ubuf.at[place, side], usem.at[place, side]).wait()

        @pl.when(i >= begin + 2)
        def _():
            store(i - 2, slot).wait()

        half = BLOCK // 2
        halves = []
        for part in range(2):
            scores = lax.dot_general(
                ubuf[place, 0],
                ubuf[place, 1, pl.ds(part * half, half), :],
                (((1,), (1,)), ((), ())),
                preferred_element_type=jnp.float32,
            )
            power = scores * (SHARPNESS * LOG2E)
            halves.append((jnp.exp2(power - 1.0) - jnp.exp2(-1.0 - power)).astype(jnp.bfloat16))
        aff = jnp.concatenate(halves, axis=1)
        affbuf[slot] = aff
        store(i, slot).start()
        add_products(pan, acc, aff, items[0, i], items[1, i])

    for back in (2, 1):

        @pl.when(end - back >= begin)
        def _():
            store(end - back, (end - back) % 2).wait()

    if final:
        write_sums(acc, joint, own, backs)


def sum_shapes(sends, per, width):
    return [jax.ShapeDtypeStruct((per, width, BLOCK), jnp.float32)] + [
        jax.ShapeDtypeStruct((per, width, BLOCK), jnp.bfloat16)
    ] * sends


def pair_call(items, bounds, stage, units, held_at, panels, state, n_slab, joint, per, width, top, final):
    held = 1 + sum(len(group) for group in joint)
    blocks = held * per
    depth = units[0].shape[1]
    per_row = depth // BLOCK
    smem = pl.BlockSpec(memory_space=pltpu.SMEM)
    hbm = pl.BlockSpec(memory_space=pltpu.HBM)
    vmem = pl.BlockSpec(memory_space=pltpu.VMEM)
    acc_shape = jax.ShapeDtypeStruct((blocks, width, BLOCK), jnp.float32)
    pan_shape = jax.ShapeDtypeStruct((per_row, blocks * width // per_row, BLOCK), jnp.bfloat16)
    aff_shape = jax.ShapeDtypeStruct((top, BLOCK, BLOCK), jnp.bfloat16)
    operands = [items, bounds, *units]
    in_specs = [smem, smem] + [hbm] * len(units)
    scratch, aliases = [], {}
    if stage == 0:
        operands += panels
        in_specs += [pl.BlockSpec(memory_space=pl.ANY)] * len(panels)
        out_shape, out_specs = [acc_shape, pan_shape, aff_shape], [vmem, vmem, hbm]
    else:
        acc, aff, pan = state
        aff_at = len(operands) + 1
        operands += [acc, aff, pan]
        in_specs += [vmem, hbm, vmem]
        if final:
            out_shape = sum_shapes(len(joint), per, width) + [aff_shape]
            out_specs = [vmem] * (1 + len(joint)) + [hbm]
            scratch = [pltpu.VMEM(acc_shape.shape, jnp.float32)]
        else:
            out_shape, out_specs = [acc_shape, aff_shape], [vmem, hbm]
        aliases = {aff_at: len(out_shape) - 1}
    return pl.pallas_call(
        functools.partial(pair_kernel, stage, held_at, n_slab, joint, per, final),
        out_shape=out_shape,
        in_specs=in_specs,
        out_specs=out_specs,
        scratch_shapes=scratch
        + [
            pltpu.VMEM((RING, 2, BLOCK, depth), jnp.bfloat16),
            pltpu.VMEM((2, BLOCK, BLOCK), jnp.bfloat16),
            pltpu.SemaphoreType.DMA((RING, 2)),
            pltpu.SemaphoreType.DMA((held * per_row,)),
            pltpu.SemaphoreType.DMA((2,)),
        ],
        input_output_aliases=aliases,
        compiler_params=pltpu.CompilerParams(vmem_limit_bytes=VMEM_LIMIT),
        name="pairs",
    )(*operands)


def apply_kernel(joint, items, bounds, *refs):
    n_panel = len(joint) + 1
    panels, refs = refs[:n_panel], refs[n_panel:]
    aff_in, own, backs, refs = refs[0], refs[1], refs[2 : n_panel + 1], refs[n_panel + 1 :]
    acc, pan, affbuf, psem, asem = refs
    end = bounds[bounds.shape[0] - 1]

    def load(i, slot):
        return pltpu.make_async_copy(aff_in.at[i], affbuf.at[slot], asem.at[slot])

    for ahead in range(APPLY_RING - 1):

        @pl.when(ahead < end)
        def _():
            load(ahead, ahead).start()

    copies = fill_panel(panels, joint, pan, psem)
    acc[...] = jnp.zeros_like(acc)
    for copy in copies:
        copy.wait()

    @pl.loop(0, end)
    def _(i):
        slot = i % APPLY_RING

        @pl.when(i + APPLY_RING - 1 < end)
        def _():
            load(i + APPLY_RING - 1, (i + APPLY_RING - 1) % APPLY_RING).start()

        load(i, slot).wait()
        add_products(pan, acc, affbuf[slot], items[0, i], items[1, i])

    write_sums(acc, joint, own, backs)


def apply_call(items, bounds, panels, joint, aff, per, width):
    held = 1 + sum(len(group) for group in joint)
    blocks = held * per
    per_row = panels[0].shape[1] // BLOCK
    smem = pl.BlockSpec(memory_space=pltpu.SMEM)
    anywhere = pl.BlockSpec(memory_space=pl.ANY)
    return pl.pallas_call(
        functools.partial(apply_kernel, joint),
        out_shape=sum_shapes(len(joint), per, width),
        in_specs=[smem, smem] + [anywhere] * len(panels) + [pl.BlockSpec(memory_space=pltpu.HBM)],
        out_specs=[pl.BlockSpec(memory_space=pltpu.VMEM)] * len(panels),
        scratch_shapes=[
            pltpu.VMEM((blocks, width, BLOCK), jnp.float32),
            pltpu.VMEM((per_row, blocks * width // per_row, BLOCK), jnp.bfloat16),
            pltpu.VMEM((APPLY_RING, BLOCK, BLOCK), jnp.bfloat16),
            pltpu.SemaphoreType.DMA((held * per_row,)),
            pltpu.SemaphoreType.DMA((APPLY_RING,)),
        ],
        compiler_params=pltpu.CompilerParams(vmem_limit_bytes=50 * 1024 * 1024),
        name="apply",
    )(items, bounds, *panels, aff)


def gram_kernel(n_back, own, *refs):
    backs, (y_out, gram_out) = refs[:n_back], refs[n_back:]
    gram = None
    for b in range(own.shape[0]):
        total = own[b]
        for back in backs:
            total = total + back[b].astype(jnp.float32)
        y_out[b] = total
        part = lax.dot_general(
            total,
            total,
            (((1,), (1,)), ((), ())),
            preferred_element_type=jnp.float32,
            precision=lax.Precision.HIGHEST,
        )
        gram = part if gram is None else gram + part
    gram_out[...] = gram


def gram_call(own, backs):
    width = own.shape[1]
    return pl.pallas_call(
        functools.partial(gram_kernel, len(backs)),
        out_shape=(
            jax.ShapeDtypeStruct(own.shape, jnp.float32),
            jax.ShapeDtypeStruct((width, width), jnp.float32),
        ),
        compiler_params=pltpu.CompilerParams(vmem_limit_bytes=VMEM_LIMIT),
        name="gram",
    )(own, *backs)


def inverse_factor(gram):
    width = gram.shape[0]
    row_id = lax.broadcasted_iota(jnp.int32, (width, width), 0)
    col_id = lax.broadcasted_iota(jnp.int32, (width, width), 1)
    table = jnp.concatenate([gram, (row_id == col_id).astype(jnp.float32)], axis=1)
    tile = 8
    tiles = [table[at : at + tile] for at in range(0, width, tile)]
    shape = tiles[0].shape
    inner = lax.broadcasted_iota(jnp.int32, shape, 0)
    scales = [None] * len(tiles)
    for k in range(0, width, 2):
        home, at = k // tile, k % tile
        line0, line1 = tiles[home][at : at + 1], tiles[home][at + 1 : at + 2]
        cols0 = {g: jnp.broadcast_to(tiles[g][:, k : k + 1], shape) for g in range(home, len(tiles))}
        cols1 = {g: jnp.broadcast_to(tiles[g][:, k + 1 : k + 2], shape) for g in range(home, len(tiles))}
        a = cols0[home][at : at + 1]
        b = cols0[home][at + 1 : at + 2]
        c = cols1[home][at + 1 : at + 2]
        inv_a = 1.0 / a
        inv_s = a / (a * c - b * b)
        line1 = line1 - (b * inv_a) * line0
        line0 = inv_a * line0
        for g in range(home, len(tiles)):
            first = cols0[g] * line0
            second = ((cols1[g] - cols0[g] * (b * inv_a)) * inv_s) * line1
            if g == home:
                first = jnp.where(inner > at, first, 0.0)
                second = jnp.where(inner > at + 1, second, 0.0)
                old = scales[g] if at else jnp.zeros(shape, jnp.float32)
                scales[g] = jnp.where(inner == at, inv_a, jnp.where(inner == at + 1, inv_s, old))
            tiles[g] = tiles[g] - first - second
    return jnp.concatenate([t[:, width:] * jnp.sqrt(z[:, :width]) for t, z in zip(tiles, scales)], axis=0)


def panel_kernel(rows_all, last, n_gram, *refs):
    grams, (y, out) = refs[:n_gram], refs[n_gram:]
    gram = grams[0][...]
    for other in grams[1:]:
        gram = gram + other[...]
    inverse = inverse_factor(gram * (1.0 / rows_all))
    for b in range(y.shape[0]):
        block = lax.dot_general(
            inverse,
            y[b],
            (((1,), (0,)), ((), ())),
            preferred_element_type=jnp.float32,
            precision=lax.Precision.HIGHEST,
        )
        if last:
            out[:, b * BLOCK : (b + 1) * BLOCK] = block
        else:
            per_row = out.shape[1] // BLOCK
            high = block.shape[0] // per_row
            for q in range(per_row):
                out[b * high : (b + 1) * high, q * BLOCK : (q + 1) * BLOCK] = block[
                    q * high : (q + 1) * high
                ].astype(jnp.bfloat16)


def panel_call(grams, y, rows_all, depth, last):
    blocks, width, _ = y.shape
    shape = (
        jax.ShapeDtypeStruct((width, blocks * BLOCK), jnp.float32)
        if last
        else jax.ShapeDtypeStruct((width * blocks * BLOCK // depth, depth), jnp.bfloat16)
    )
    return pl.pallas_call(
        functools.partial(panel_kernel, rows_all, last, len(grams)),
        out_shape=shape,
        compiler_params=pltpu.CompilerParams(vmem_limit_bytes=VMEM_LIMIT),
        name="panel",
    )(*grams, y)


def sum_over_rows(value):
    count = lax.axis_size("rows")
    terms, step = [value], 1
    while step < count:
        value = functools.reduce(jnp.add, terms)
        radix = min(4, count // step)
        terms = [value] + [
            lax.ppermute(value, "rows", [(i, i ^ (step * m)) for i in range(count)]) for m in range(1, radix)
        ]
        step *= radix
    return terms


def on_device(embeddings, block_pairs, pair_count, start_panel):
    count = lax.axis_size("rows")
    me = lax.axis_index("rows")
    depth = embeddings.shape[1]
    per = embeddings.shape[0] // BLOCK
    width = start_panel.shape[0]
    slots = block_pairs.shape[0]
    moves, via, after_back, hops, joint, hold, place, work, late, light, settle, bare, after, top = make_plan(count)
    held = len(moves) + 1

    merged = [functools.reduce(list.__add__, [moves[s - 1] for s in group]) for group in joint]

    direct = [
        [(int(hold[w, s]), w) for s in group for w in range(count) if hold[w, s] >= 0] for group in joint
    ]

    def spread(value):
        got = [value]
        for group, pairs in zip(joint, merged):
            got.append(lax.ppermute(got[via.get(group[0], 0)], "rows", pairs))
        return got

    assert count * per <= 256
    extra = extra_call(block_pairs.T, pair_count, start_panel, depth)
    ahead = {g: lax.ppermute(extra, "rows", direct[g]) for g, group in enumerate(joint) if group[0] in light}
    *alone, packed = pack_call(embeddings, extra, bare)
    units = {0: packed}
    for m in range(1, len(moves) + 1):
        outgoing = alone[0] if m in light and bare else packed
        if m in settle:
            outgoing, ahead = lax.optimization_barrier((outgoing, ahead))
        if m in via:
            outgoing = units[via[m]]
        if m in after:
            outgoing, _ = lax.optimization_barrier((outgoing, units[after[m]]))
        for pairs in hops.get(m, [moves[m - 1]]):
            outgoing = lax.ppermute(outgoing, "rows", pairs)
        units[m] = outgoing
    early = [m for m in range(held) if m not in late]
    tails = {m: units[m] for m in early if m not in light}
    n_slab = len(tails)
    tails.update({m: ahead[g] for g in ahead for m in joint[g]})
    lists = jnp.stack(
        [tails[m][tails[m].shape[0] - LIST_ROWS, : 2 * slots + 1].astype(jnp.int32) for m in range(held)]
    )
    items, bounds = work_list(lists, hold, place, work, late, slots, per, top, me)

    order = early + sorted(late)
    held_at = [(m * per, per) for m in order]
    rows_of = [units[m] for m in order]
    shape = (n_slab, joint, per, width, top)
    n_early = len(early)
    acc, pan, aff = pair_call(
        items, bounds, 0, rows_of[:n_early], held_at[:n_early], list(ahead.values()), None, *shape, False
    )
    *sums, aff = pair_call(items, bounds, 1, rows_of, held_at, None, (acc, aff, pan), *shape, True)

    for sweep in range(ITERS):
        if sweep > 0:
            sums = apply_call(items, bounds, spread(panel), joint, aff, per, width)
        sums, backs, gone = list(sums), [], {}
        for m in sorted(range(1, len(joint) + 1), key=lambda m: m not in via):
            outgoing = sums[m]
            if m in after_back:
                outgoing, _ = lax.optimization_barrier((outgoing, gone[after_back[m]]))
            back = lax.ppermute(outgoing, "rows", [(target, source) for source, target in merged[m - 1]])
            gone[m] = back
            if m in via:
                sums[via[m]] = sums[via[m]] + back
            else:
                backs.append(back)
        y, gram = gram_call(sums[0], backs)
        grams = sum_over_rows(gram)
        panel = panel_call(grams, y, count * embeddings.shape[0], depth, sweep == ITERS - 1)
    return panel


def solution(mesh):
    in_specs = (
        P(("groups", "rows"), None),
        P(("groups", "rows"), None),
        P(("groups", "rows")),
        P(None, ("groups", "rows")),
    )
    out_specs = P(None, ("groups", "rows"))
    return jax.shard_map(on_device, mesh=mesh, in_specs=in_specs, out_specs=out_specs, check_vma=False)
```
